512 devices in a mesh: tile: 128 (over y, z, core), mem: 4 (over x).
Axes of the slice: x: 4, y: 8, z: 8, core: 2. Of those that a mesh axis runs over, the one named last changes fastest.
Arguments:
- radiance: bfloat16 [3072, 80, 4352], P('tile', 'mem'), may hold values from -6 to 6
- observed: bfloat16 [3072, 4352], P('tile', 'mem'), may hold values from -6 to 6
- basis: bfloat16 [4352, 300], P('mem'), may hold values from -0.09375 to 0.09375
- precision_pc: float32 [300], replicated, may hold values from 0.002 to 0.02
- tile_lists: int32 [3072, 3], P('tile'), may hold values from 0 to 127, all different within a row; in each aligned block of 24 rows (0 to 23, 24 to 47, ...) at most 2 rows name the same one
- radius_bins: int32 [3072, 3], P('tile'), may hold values from 0 to 7
Outputs:
- analysis: bfloat16 [3072, 80, 300], P('tile', 'mem')
The draws below stay inside these ranges and needn't reach their ends.
Inputs may be any that keep to these rules, and one draw needn't show every extreme that they name: `tile_lists`: each row names 3 different tiles; within the rows of one swath no tile is named more than 2 times.
All inputs are finite; a program needn't handle non-finite values. Where the reference program divides by a largest or mean magnitude, that divisor is 1e-20 or more.
Results may differ from the reference program's by a relative error of at most 0.0011.
The reference program's roundings to bfloat16 on the way (of `innovation`, `perturbed`, `rounded_loc` and `weighted`) count: a program that leaves them out, or rounds other values in their place, can miss the bound.
Values may be sent and summed in bfloat16 or wider, within the bound.
No kernel may reach another device: no remote copies, remote signals or barrier semaphores. Data moves between devices by JAX's collectives and lax.ppermute only.
A program may use at most 128 MiB of HBM per device.

```python
import math
import jax
import jax.numpy as jnp
import numpy as np
from jax import lax

MEMBERS = 80
CHANNELS = 4352
PCS = 300
OBS_DEV = 24
TOP = 3
NS_ITERS = 4
OBS = 3072
CAP = 2
N_TILE = 128


def plant(entries, key, low, top_value):
    dims = entries.shape
    spot = [jax.random.randint(jax.random.fold_in(key, axis), (), 0, dims[axis]) for axis in range(len(dims))]
    entries = entries.at[tuple(spot)].set(low)
    longest = dims.index(max(dims))
    spot[longest] = (spot[longest] + 1) % dims[longest]
    return entries.at[tuple(spot)].set(top_value)


def level_of(key, shape, pieces, smallest, top_value):
    loudness, own = 1.0, jax.random.fold_in(key, 6)
    for axis_at, shards_of in pieces:
        draws = jnp.exp(jax.random.uniform(jax.random.fold_in(own, axis_at), (shards_of,), jnp.float32, smallest / len(pieces), top_value / len(pieces)))
        loudness = loudness * jnp.repeat(draws, shape[axis_at] // shards_of).reshape([-1 if axis == axis_at else 1 for axis in range(len(shape))])
    return loudness


def shared_out(rng, own, number, rows, amount, top, most, lean):
    sequence = jax.random.permutation(rng, amount)
    crowded, usual = load_shares(amount, rows * top, most, lean, True), load_shares(amount, rows * top, most, lean, False)
    places = jnp.arange(amount)

    def named(tallies, turn):
        used = int((tallies > 0).sum())
        fixed = max(1, used // 4)
        moved = fixed + (places - fixed + turn * (used - fixed)) % max(1, amount - fixed)
        return jnp.zeros((amount,), jnp.int32).at[sequence[jnp.where(places < fixed, places, moved)]].set(jnp.asarray(tallies, jnp.int32))

    tallies = jnp.where(number % 4 == 0, named(crowded, number // 4), named(usual, number - number // 4 - 1))
    mixed = jax.random.permutation(jax.random.fold_in(own, 3), amount)
    source_of, receiver = mixed[0:amount // 2 * 2:2], mixed[1:amount // 2 * 2:2]
    room = jnp.minimum(tallies[source_of] - 1, most - tallies[receiver]) // 2
    room = jnp.where((source_of == sequence[0]) | (receiver == sequence[0]) | (tallies[receiver] == 0), 0, jnp.maximum(room, 0))
    moved = jax.random.randint(jax.random.fold_in(own, 4), (amount // 2,), 0, 1 << 20) % (room + 1)
    tallies = tallies.at[source_of].add(-moved).at[receiver].add(moved)
    items = jnp.searchsorted(jnp.cumsum(tallies), jnp.arange(rows * top), side="right").astype(jnp.int32)
    listing = items.reshape(top, rows).T
    listing = listing[jax.random.permutation(jax.random.fold_in(own, 1), rows)]
    turn = jax.random.randint(jax.random.fold_in(own, 2), (rows, 1), 0, top)
    return jnp.take_along_axis(listing, (jnp.arange(top)[None, :] + turn) % top, axis=1)


def load_shares(count, total, most, skew, full):
    portions = [(1 << 20) // math.isqrt(standing ** skew) + 1 for standing in range(1, count + 1)]
    largest = most if full else min(most, max(-(-total // count), total * portions[0] // sum(portions)))
    least = 1 if total - largest >= count - 1 else 0
    counts, rest = [largest] + [least] * (count - 1), total - largest - least * (count - 1)
    while rest > 0:
        movable = [i for i in range(1, count) if counts[i] < largest] or [i for i in range(1, count) if counts[i] < most]
        pool, budget = sum([portions[i] for i in movable]), rest
        for i in movable:
            extra = min(most - counts[i], max(1, budget * portions[i] // pool), rest)
            counts[i] = counts[i] + extra
            rest = rest - extra
    return np.array(counts)


def normal_values(key, extent, width, limit, pieces=(), kind=jnp.bfloat16):
    drawn = width * jax.random.normal(key, extent, jnp.float32)
    if pieces:
        drawn = drawn * level_of(key, extent, pieces, -0.22, 0.18)
    return jnp.clip(drawn, -limit, limit).astype(kind)


def setup_inputs(seed: int = 0) -> dict:
    key_of = jax.random.split(jax.random.key(seed), 7)
    radiance = normal_values(key_of[0], (OBS, MEMBERS, CHANNELS), 1.0, 6.0, ((0, 128), (1, 4)))
    observed = normal_values(key_of[1], (OBS, CHANNELS), 1.0, 6.0, ((0, 128), (1, 4)))
    basis = normal_values(key_of[2], (CHANNELS, PCS), CHANNELS ** -0.5, 0.09375, ((0, 4),))
    precision_pc = jnp.clip(jnp.exp(jax.random.uniform(key_of[3], (PCS,), jnp.float32, math.log(0.002), math.log(0.02))), 0.002, 0.02)
    tile_lists_keys = jax.random.split(jax.random.fold_in(key_of[4], 1), OBS // OBS_DEV)
    tile_lists_turns = jax.random.permutation(jax.random.fold_in(key_of[4], 3), OBS // OBS_DEV)
    tile_lists = jax.vmap(lambda own, number: shared_out(jax.random.fold_in(key_of[4], 2), own, number, OBS_DEV, N_TILE, TOP, CAP, 2))(tile_lists_keys, tile_lists_turns).reshape((OBS, TOP))
    radius_bins = plant(jax.random.randint(key_of[5], (OBS, TOP), 0, 8), jax.random.fold_in(key_of[5], 1), 0, 7).astype(jnp.int32)
    return dict(radiance=radiance, observed=observed, basis=basis, precision_pc=precision_pc, tile_lists=tile_lists, radius_bins=radius_bins)


bin_spread = 3.0

def localization(radius_bins):
    scaled = radius_bins.astype(jnp.float32) / bin_spread
    return jnp.exp(-0.5 * scaled * scaled)

def square_root_weights(gram, pull):
    highest = lax.Precision.HIGHEST
    order = gram.shape[0]
    identity = jnp.eye(order, dtype=jnp.float32)
    symmetric = 0.5 * (gram + gram.T)
    scaled = identity + symmetric / (order - 1.0)
    bound = jnp.max(lax.optimization_barrier(jnp.sum(jnp.abs(scaled), axis=1)))
    root_iter = scaled / bound
    inverse_iter = identity
    for sweep in range(NS_ITERS):
        factor = 1.5 * identity - 0.5 * jnp.dot(inverse_iter, root_iter, precision=highest)
        root_iter = jnp.dot(root_iter, factor, precision=highest)
        inverse_iter = jnp.dot(factor, inverse_iter, precision=highest)
    spread = inverse_iter / jnp.sqrt(bound)
    inverse = jnp.dot(inverse_iter, inverse_iter, precision=highest) / (bound * (order - 1.0))
    offset = jnp.dot(inverse, pull, precision=highest)
    return spread + offset[:, None]

def reference(radiance, observed, basis, precision_pc, tile_lists, radius_bins):
    highest = lax.Precision.HIGHEST
    obs_total, members, channels = radiance.shape
    components = basis.shape[1]
    fanout = tile_lists.shape[1]
    scores = jnp.dot(radiance.reshape(obs_total * members, channels), basis, preferred_element_type=jnp.float32).reshape(obs_total, members, components)
    obs_score = jnp.dot(observed, basis, preferred_element_type=jnp.float32)
    member_mean = lax.optimization_barrier(jnp.sum(scores, axis=1)) / members
    innovation = (obs_score - member_mean).astype(jnp.bfloat16)
    perturbed = (scores - member_mean[:, None, :]).astype(jnp.bfloat16)
    weights_loc = localization(radius_bins)
    rounded_loc = weights_loc.astype(jnp.bfloat16)
    per_block = obs_total // N_TILE
    tile_ids = jnp.arange(N_TILE, dtype=jnp.int32)

    def accumulate(carry, block):
        gram_all, pull_all = carry
        block_pert, block_innov, block_loc, block_dest = block
        for slot_r in range(fanout):
            factor = block_loc[:, slot_r].astype(jnp.float32)[:, None] * precision_pc[None, :]
            weighted = (block_pert.astype(jnp.float32) * factor[:, None, :]).astype(jnp.bfloat16)
            gram_terms = jnp.einsum('okp,omp->okm', weighted.astype(jnp.float32), block_pert.astype(jnp.float32), precision=highest)
            pull_terms = jnp.einsum('okp,op->ok', weighted.astype(jnp.float32), block_innov.astype(jnp.float32), precision=highest)
            onehot = (block_dest[:, slot_r][:, None] == tile_ids[None, :]).astype(jnp.float32)
            gram_all = gram_all + jnp.einsum('ot,okm->tkm', onehot, gram_terms, precision=highest)
            pull_all = pull_all + jnp.einsum('ot,ok->tk', onehot, pull_terms, precision=highest)
        return ((gram_all, pull_all), None)
    blocks = (perturbed.reshape(N_TILE, per_block, members, components), innovation.reshape(N_TILE, per_block, components), rounded_loc.reshape(N_TILE, per_block, fanout), tile_lists.reshape(N_TILE, per_block, fanout))
    start = (jnp.zeros((N_TILE, members, members), jnp.float32), jnp.zeros((N_TILE, members), jnp.float32))
    (gram_all, pull_all), unused = lax.scan(accumulate, start, blocks)
    tile_weights = jax.vmap(square_root_weights)(gram_all, pull_all)
    coef = weights_loc / lax.optimization_barrier(jnp.sum(weights_loc, axis=1, keepdims=True))
    blended = jnp.zeros((obs_total, members, members), jnp.float32)
    for slot_r in range(fanout):
        blended = blended + coef[:, slot_r][:, None, None] * tile_weights[tile_lists[:, slot_r]]
    mixed = jnp.einsum('omp,omk->okp', perturbed.astype(jnp.float32), blended, precision=highest)
    return (member_mean[:, None, :] + mixed).astype(jnp.bfloat16)
```

```python
import jax
import jax.numpy as jnp
from jax import lax
from jax.experimental import pallas as pl
from jax.experimental.pallas import tpu as pltpu
from jax.sharding import Mesh, PartitionSpec as P

NS_ITERS = 4
bin_spread = 3.0

GROUPS = 4
MEM = 20
OBS = 24
TOP = 3
COMPS = 300
WIDE = 384
ROWS = 304
HALF = 160
SPAN = 96
BLOCK = 1088
FRAME = 1152
CHIPS = 64

F32 = jnp.float32
BF16 = jnp.bfloat16
HIGHEST = lax.Precision.HIGHEST
NT = (((1,), (1,)), ((), ()))
VMEM = pl.BlockSpec(memory_space=pltpu.VMEM)
SMEM = pl.BlockSpec(memory_space=pltpu.SMEM)
ANY = pl.BlockSpec(memory_space=pl.ANY)


def params():
    return pltpu.CompilerParams(vmem_limit_bytes=32 * 1024 * 1024)


def localization(radius_bins):
    scaled = radius_bins.astype(F32) / bin_spread
    return jnp.exp(-0.5 * scaled * scaled)


def frame_of(block):
    return pl.multiple_of(1024 * block + 128 * lax.div(block, 2), 128)


def own_kernel(place, rad, own, out):
    columns = pl.ds(frame_of(place[0]), FRAME)
    out[...] = lax.dot_general(rad[:, columns], own[...], NT, preferred_element_type=F32)


def own_call(place, rad, own):
    return pl.pallas_call(
        own_kernel,
        out_shape=jax.ShapeDtypeStruct((MEM * OBS, ROWS), F32),
        in_specs=[SMEM, VMEM, VMEM],
        out_specs=VMEM,
        compiler_params=params(),
        name="scores_own",
    )(place, rad, own)


def scores_kernel(place, rad, first, beside1, beside2, far1, far2, out, total, far):
    group, core = place[0], place[1]
    near = pl.ds(pl.multiple_of(core * (ROWS - HALF), 16), HALF)
    far[near, :] = far1[...]
    rest = ROWS - HALF
    source = pl.ds(pl.multiple_of((1 - core) * (HALF - rest), 16), rest)
    target = pl.ds(pl.multiple_of((1 - core) * HALF, 16), rest)
    far[target, :] = far2[source, :]
    step = 2 * core - 1
    blocks = (
        (beside1, lax.rem(group + step + GROUPS, GROUPS)),
        (beside2, lax.rem(group - step + GROUPS, GROUPS)),
        (far, lax.rem(group + 2, GROUPS)),
    )
    members = 10
    rows = members * OBS
    sums = jnp.zeros((OBS, ROWS), F32)
    for part in range(MEM // members):
        span = slice(part * rows, (part + 1) * rows)
        acc = first[span, :]
        for block, index in blocks:
            acc = acc + lax.dot_general(
                rad[span, pl.ds(frame_of(index), FRAME)],
                block[...],
                NT,
                preferred_element_type=F32,
            )
        block = acc.reshape(members, OBS, ROWS)
        out[part * members : (part + 1) * members, :, :] = block
        sums = sums + jnp.sum(block, axis=0)
    total[...] = sums


def scores_call(place, rad, first, beside1, beside2, far1, far2):
    return pl.pallas_call(
        scores_kernel,
        out_shape=(
            jax.ShapeDtypeStruct((MEM, OBS, ROWS), F32),
            jax.ShapeDtypeStruct((OBS, ROWS), F32),
        ),
        in_specs=[SMEM] + [VMEM] * 6,
        out_specs=(VMEM, VMEM),
        scratch_shapes=[pltpu.VMEM((ROWS, FRAME), BF16)],
        compiler_params=params(),
        name="scores",
    )(place, rad, first, beside1, beside2, far1, far2)


def widen(value):
    return jnp.concatenate([value, jnp.zeros(value.shape[:-1] + (WIDE - ROWS,), F32)], axis=-1)


def perturb_kernel(scores, totals1, totals2, out, innovation, mean):
    totals = totals1[...] + totals2[...]
    average = totals[0] / (GROUPS * MEM)
    mean[...] = widen(average)
    innovation[...] = widen(totals[1] - average).astype(BF16)
    for m in range(MEM):
        out[m, :, :] = widen(scores[m] - average).astype(BF16)


def perturb_call(scores, totals1, totals2):
    return pl.pallas_call(
        perturb_kernel,
        out_shape=(
            jax.ShapeDtypeStruct((MEM, OBS, WIDE), BF16),
            jax.ShapeDtypeStruct((OBS, WIDE), BF16),
            jax.ShapeDtypeStruct((OBS, WIDE), F32),
        ),
        in_specs=[VMEM] * 3,
        out_specs=(VMEM,) * 3,
        compiler_params=params(),
        name="perturb",
    )(scores, totals1, totals2)


def gram_kernel(place, targets, loc, precision, innov, own, p1, p2, p3, keep, send, every, rows, acc):
    core = place[1]
    rows[...] = jnp.zeros_like(rows)
    acc[...] = jnp.zeros_like(acc)
    for at, block in ((0, own), (MEM, p1), (2 * MEM, p2), (3 * MEM + 1, p3)):
        for m in range(MEM):
            wide = block[m].astype(F32)
            for g in range(OBS // 8):
                for lane in range(WIDE // 128):
                    rows[lane, pl.ds(g * 8 * SPAN + at + m, 8, stride=SPAN), :] = wide[
                        g * 8 : g * 8 + 8, lane * 128 : lane * 128 + 128
                    ]
    wide = innov[...].astype(F32)
    for g in range(OBS // 8):
        for lane in range(WIDE // 128):
            rows[lane, pl.ds(g * 8 * SPAN + 3 * MEM, 8, stride=SPAN), :] = wide[
                g * 8 : g * 8 + 8, lane * 128 : lane * 128 + 128
            ]
    live = lax.broadcasted_iota(jnp.int32, (24, 128), 0) < MEM
    fade = [
        jnp.where(live, precision[0:1, lane * 128 : lane * 128 + 128], 0.0)
        for lane in range(WIDE // 128)
    ]

    def footprint(o, carry):
        start = pl.multiple_of(o * SPAN, SPAN)
        result = None
        for lane in range(WIDE // 128):
            whole = rows[lane, pl.ds(start, SPAN), :]
            every[o, :, lane * 128 : lane * 128 + 128] = whole.astype(BF16)
            mine = whole[:24]
            weighted = jnp.concatenate(
                [mine * (loc[o * TOP + r] * fade[lane]) for r in range(TOP)], axis=0
            ).astype(BF16)
            right = jnp.concatenate([whole[:64], jnp.zeros((64, 128), F32)], axis=0).astype(BF16)
            term = lax.dot_general(weighted, right, NT, preferred_element_type=F32)
            result = term if result is None else result + term
        for r in range(TOP):
            target = targets[o * TOP + r]
            bit = lax.rem(target, 2)
            side = bit + core - 2 * bit * core
            index = side * CHIPS + lax.div(target, 2)
            part = result[24 * r : 24 * r + 24]
            acc[index, 0:8, :] += part[0:8] + pltpu.roll(part[16:24], 64, 1)
            acc[index, 8:16, :] += part[8:16]
        return carry

    lax.fori_loop(0, OBS, footprint, 0, unroll=4)
    keep[...] = acc[:CHIPS]
    send[...] = acc[CHIPS:]


def gram_call(place, targets, loc, precision, innov, own, p1, p2, p3):
    half = jax.ShapeDtypeStruct((CHIPS, 16, 128), F32)
    return pl.pallas_call(
        gram_kernel,
        out_shape=(half, half, jax.ShapeDtypeStruct((OBS, SPAN, WIDE), BF16)),
        in_specs=[SMEM] * 3 + [VMEM] * 6,
        out_specs=(VMEM,) * 3,
        scratch_shapes=[
            pltpu.VMEM((WIDE // 128, OBS * SPAN, 128), F32),
            pltpu.VMEM((2 * CHIPS, 16, 128), F32),
        ],
        compiler_params=params(),
        name="gram",
    )(place, targets, loc, precision, innov, own, p1, p2, p3)


def root_kernel(place, gathered, out, upper):
    group = place[0]
    order = GROUPS * MEM
    lane20 = lax.broadcasted_iota(jnp.int32, (MEM, 128), 1)
    share = jnp.where(lane20 < 20, 0.5, jnp.where(lane20 < 40, 1.0, jnp.where(lane20 < 60, 0.5, 0.0)))
    upper[...] = jnp.zeros_like(upper)
    for d in range(GROUPS):
        block = gathered[lax.rem(group + d, GROUPS)]
        full = jnp.concatenate([block, pltpu.roll(block[0:8], 64, 1)[0:4]], axis=0)
        scaled = full * share
        shift = MEM * d
        placed = scaled if d == 0 else pltpu.roll(scaled, shift, 1)
        placed = jnp.where(lane20 < order, placed, 0.0)
        if d >= 2:
            wrapped = pltpu.roll(scaled, (shift - order) % 128, 1)
            placed = placed + jnp.where(lane20 < shift - 20, wrapped, 0.0)
        placed = placed + jnp.where(lane20 == order, pltpu.roll(full, 20, 1), 0.0)
        upper[shift : shift + MEM, :] = placed
    half = upper[...]
    flipped = half.T
    row = lax.broadcasted_iota(jnp.int32, (128, 128), 0)
    lane = lax.broadcasted_iota(jnp.int32, (128, 128), 1)
    inside = (row < order) & (lane < order)
    identity = jnp.where(inside & (row == lane), 1.0, 0.0)
    symmetric = jnp.where(inside, half + flipped, 0.0)
    matrix = identity + symmetric / (order - 1.0)
    bound = jnp.max(jnp.sum(jnp.abs(matrix), axis=1, keepdims=True), axis=0, keepdims=True)
    pull = flipped[order : order + 8]
    pull = jnp.where(
        (lax.broadcasted_iota(jnp.int32, (8, 128), 1) < order)
        & (lax.broadcasted_iota(jnp.int32, (8, 128), 0) == 0),
        pull,
        0.0,
    )

    def times(a, b):
        return jnp.dot(a, b, precision=HIGHEST, preferred_element_type=F32)

    root = matrix / bound
    inverse = None
    for sweep in range(NS_ITERS):
        product = root if inverse is None else times(inverse, root)
        factor = 1.5 * identity - 0.5 * product
        if sweep < NS_ITERS - 1:
            root = times(root, factor)
        inverse = factor if inverse is None else times(factor, inverse)
    offset = times(times(pull, inverse), inverse) / (bound * (order - 1.0))
    weights = inverse[0:24] / jnp.sqrt(bound) + offset[0:1]
    lane8 = lax.broadcasted_iota(jnp.int32, (8, 128), 1)
    row8 = lax.broadcasted_iota(jnp.int32, (8, 128), 0)
    tail = jnp.where(row8 < 4, weights[16:24], 0.0)
    first = jnp.where(lane8 >= 80, pltpu.roll(tail, 80, 1), 0.0)
    second = jnp.where((lane8 >= 80) & (lane8 < 112), pltpu.roll(tail, 32, 1), 0.0)
    out[0:8, :] = weights[0:8] + first + pltpu.roll(second, 4, 0)
    out[8:16, :] = weights[8:16]


def root_call(place, gathered):
    return pl.pallas_call(
        root_kernel,
        out_shape=jax.ShapeDtypeStruct((16, 128), F32),
        in_specs=[SMEM, VMEM],
        out_specs=VMEM,
        scratch_shapes=[pltpu.VMEM((128, 128), F32)],
        compiler_params=params(),
        name="root",
    )(place, gathered)


def mix_kernel(place, targets, coef, mine, other, every, mean, out, rows):
    core = place[1]
    lane8 = lax.broadcasted_iota(jnp.int32, (8, 128), 1)
    row8 = lax.broadcasted_iota(jnp.int32, (8, 128), 0)

    def footprint(o, carry):
        blend = jnp.zeros((16, 128), F32)
        for r in range(TOP):
            target = targets[o * TOP + r]
            index = lax.div(target, 2)
            local = lax.rem(target, 2) == core
            piece = jnp.where(local, mine[index], other[index])
            blend = blend + coef[o * TOP + r] * piece
        top, middle = blend[0:8], blend[8:16]
        first = jnp.where(lane8 < 48, pltpu.roll(top, 48, 1), 0.0)
        second = jnp.where((lane8 >= 48) & (lane8 < 80), pltpu.roll(top, 96, 1), 0.0)
        tail = jnp.where(row8 < 4, first + pltpu.roll(second, 4, 0), 0.0)
        whole = jnp.concatenate(
            [jnp.where(lane8 < 80, top, 0.0), jnp.where(lane8 < 80, middle, 0.0), tail], axis=0
        )
        lane24 = lax.broadcasted_iota(jnp.int32, (24, 128), 1)
        moved = jnp.where((lane24 > 60) & (lane24 < 81), pltpu.roll(whole, 1, 1), 0.0)
        whole = jnp.where(lane24 < 60, whole, moved)
        high = whole.astype(BF16).astype(F32)
        both = jnp.concatenate([high, whole - high], axis=0).astype(BF16)
        pert = jnp.concatenate([every[o], jnp.zeros((128 - SPAN, WIDE), BF16)], axis=0)
        mixed = jnp.dot(both, pert, preferred_element_type=F32)
        mixed = mixed[0:24] + mixed[24:48] + mean[pl.ds(o, 1), :]
        for g in range(3):
            for lane in range(WIDE // 128):
                rows[lane, pl.ds(g * 8 * OBS + o, 8, stride=OBS), :] = mixed[
                    g * 8 : g * 8 + 8, lane * 128 : lane * 128 + 128
                ]
        return carry

    lax.fori_loop(0, OBS, footprint, 0, unroll=4)
    for m in range(MEM):
        wide = jnp.concatenate(
            [rows[lane, m * OBS : (m + 1) * OBS, :] for lane in range(WIDE // 128)], axis=1
        )
        out[m, :, :] = wide[:, :COMPS].astype(BF16)


def mix_call(place, targets, coef, mine, other, every, mean):
    return pl.pallas_call(
        mix_kernel,
        out_shape=jax.ShapeDtypeStruct((MEM, OBS, COMPS), BF16),
        in_specs=[SMEM] * 3 + [VMEM] * 4,
        out_specs=VMEM,
        scratch_shapes=[pltpu.VMEM((WIDE // 128, 24 * OBS, 128), F32)],
        compiler_params=params(),
        name="mix",
    )(place, targets, coef, mine, other, every, mean)


def shift(value, steps):
    return lax.ppermute(value, "mem", [(i, (i + steps) % GROUPS) for i in range(GROUPS)])


def swap(value):
    return lax.ppermute(value, "core", [(0, 1), (1, 0)])


def turn(value):
    pairs = [(i, (i + 1) % GROUPS) for i in range(GROUPS)]
    pairs += [(GROUPS + i, GROUPS + (i - 1) % GROUPS) for i in range(GROUPS)]
    return lax.ppermute(value, ("core", "mem"), pairs)


def pad_lanes(value, width):
    return jnp.pad(value, [(0, 0)] * (value.ndim - 1) + [(0, width - value.shape[-1])])


def body(radiance, observed, basis, precision_pc, tile_lists, radius_bins):
    group = lax.axis_index("mem")
    core = lax.axis_index("core")
    place = jnp.stack([group, core]).astype(jnp.int32)
    rad = jnp.transpose(radiance, (1, 0, 2)).reshape(MEM * OBS, GROUPS * BLOCK)

    turned = basis.T
    spare = ROWS - COMPS
    own = jnp.where(
        lax.rem(group, 2) == 1,
        jnp.pad(turned, ((0, spare), (FRAME - BLOCK, 0))),
        jnp.pad(turned, ((0, spare), (0, FRAME - BLOCK))),
    )
    beside1 = turn(own)
    first = own_call(place, rad, own)
    obs_partial = pad_lanes(jnp.dot(observed, basis, preferred_element_type=F32), ROWS)
    beside1, first, obs_partial = lax.optimization_barrier((beside1, first, obs_partial))
    far1 = turn(lax.dynamic_slice_in_dim(beside1, core * (ROWS - HALF), HALF, 0))
    beside2 = swap(beside1)
    far2 = swap(far1)
    scores, member_sum = scores_call(place, rad, first, beside1, beside2, far1, far2)
    totals = jnp.stack([member_sum, obs_partial])
    totals = totals + lax.ppermute(totals, "mem", [(0, 1), (1, 0), (2, 3), (3, 2)])
    across = lax.ppermute(totals, "mem", [(0, 3), (3, 0), (1, 2), (2, 1)])
    perturbed, innovation, mean = perturb_call(scores, totals, across)
    after1 = shift(perturbed, 3)
    after3 = shift(perturbed, 1)
    after2 = turn(jnp.where(core == 0, after3, after1))

    weights_loc = localization(radius_bins)
    rounded_loc = lax.reduce_precision(weights_loc, 8, 7).reshape(OBS * TOP)
    coef = (weights_loc / jnp.sum(weights_loc, axis=1, keepdims=True)).reshape(OBS * TOP)
    targets = tile_lists.reshape(OBS * TOP)
    keep, send, every = gram_call(
        place,
        targets,
        rounded_loc,
        pad_lanes(precision_pc[None], WIDE),
        innovation,
        perturbed,
        after1,
        after2,
        after3,
    )
    chip_sum = keep + swap(send)
    arrived = lax.all_to_all(chip_sum, ("y", "z"), split_axis=0, concat_axis=0, tiled=True)
    gathered = lax.all_gather(jnp.sum(arrived, axis=0), "mem", axis=0)
    weights = root_call(place, gathered)
    mine = lax.all_to_all(
        jnp.broadcast_to(weights[None], (CHIPS, 16, 128)),
        ("y", "z"),
        split_axis=0,
        concat_axis=0,
        tiled=True,
    )
    other = swap(mine)
    analysis = mix_call(place, targets, coef, mine, other, every, mean)
    return jnp.transpose(analysis, (1, 0, 2))


def solution(mesh):
    fine = Mesh(mesh.devices.reshape(8, 8, 2, GROUPS), ("y", "z", "core", "mem"))
    tile = ("y", "z", "core")
    placed = (
        P(tile, "mem", None),
        P(tile, "mem"),
        P("mem", None),
        P(),
        P(tile, None),
        P(tile, None),
    )
    return jax.shard_map(
        body, mesh=fine, in_specs=placed, out_specs=P(tile, "mem", None), check_vma=False
    )
```

```python
import jax
import jax.numpy as jnp
from jax import lax
from jax.experimental import pallas as pl
from jax.experimental.pallas import tpu as pltpu
from jax.sharding import Mesh, PartitionSpec as P

NS_ITERS = 4
bin_spread = 3.0

GROUPS = 4
MEM = 20
OBS = 24
TOP = 3
COMPS = 300
WIDE = 384
ROWS = 304
HALF = 160
SIDE = 51
SPAN = 96
BLOCK = 1088
FRAME = 1152
CHIPS = 64

F32 = jnp.float32
BF16 = jnp.bfloat16
HIGHEST = lax.Precision.HIGHEST
NT = (((1,), (1,)), ((), ()))
VMEM = pl.BlockSpec(memory_space=pltpu.VMEM)
SMEM = pl.BlockSpec(memory_space=pltpu.SMEM)
ANY = pl.BlockSpec(memory_space=pl.ANY)


def params():
    return pltpu.CompilerParams(vmem_limit_bytes=32 * 1024 * 1024)


def localization(radius_bins):
    scaled = radius_bins.astype(F32) / bin_spread
    return jnp.exp(-0.5 * scaled * scaled)


def frame_of(block):
    return pl.multiple_of(1024 * block + 128 * lax.div(block, 2), 128)


def own_kernel(place, rad, own, out):
    columns = pl.ds(frame_of(place[0]), FRAME)
    out[...] = lax.dot_general(rad[:, columns], own[...], NT, preferred_element_type=F32)


def own_call(place, rad, own):
    return pl.pallas_call(
        own_kernel,
        out_shape=jax.ShapeDtypeStruct((MEM * OBS, ROWS), F32),
        in_specs=[SMEM, VMEM, VMEM],
        out_specs=VMEM,
        compiler_params=params(),
        name="scores_own",
    )(place, rad, own)


def scores_kernel(place, rad, first, beside1, beside2, far1, far2, out, total, far):
    group, core = place[0], place[1]
    near = pl.ds(pl.multiple_of(core * (ROWS - HALF), 16), HALF)
    far[near, :] = far1[...]
    rest = ROWS - HALF
    source = pl.ds(pl.multiple_of((1 - core) * (HALF - rest), 16), rest)
    target = pl.ds(pl.multiple_of((1 - core) * HALF, 16), rest)
    far[target, :] = far2[source, :]
    step = 2 * core - 1
    blocks = (
        (beside1, lax.rem(group + step + GROUPS, GROUPS)),
        (beside2, lax.rem(group - step + GROUPS, GROUPS)),
        (far, lax.rem(group + 2, GROUPS)),
    )
    members = 10
    rows = members * OBS
    sums = jnp.zeros((OBS, ROWS), F32)
    for part in range(MEM // members):
        span = slice(part * rows, (part + 1) * rows)
        acc = first[span, :]
        for block, index in blocks:
            acc = acc + lax.dot_general(
                rad[span, pl.ds(frame_of(index), FRAME)],
                block[...],
                NT,
                preferred_element_type=F32,
            )
        block = acc.reshape(members, OBS, ROWS)
        out[part * members : (part + 1) * members, :, :] = block
        sums = sums + jnp.sum(block, axis=0)
    total[...] = sums


def scores_call(place, rad, first, *pieces):
    return pl.pallas_call(
        scores_kernel,
        out_shape=(
            jax.ShapeDtypeStruct((MEM, OBS, ROWS), F32),
            jax.ShapeDtypeStruct((OBS, ROWS), F32),
        ),
        in_specs=[SMEM] + [VMEM] * 6,
        out_specs=(VMEM, VMEM),
        scratch_shapes=[pltpu.VMEM((ROWS, FRAME), BF16)],
        compiler_params=params(),
        name="scores",
    )(place, rad, first, *pieces)


def widen(value):
    return jnp.concatenate([value, jnp.zeros(value.shape[:-1] + (WIDE - ROWS,), F32)], axis=-1)


def perturb_kernel(scores, parts, out, innovation, mean):
    totals = (parts[0] + parts[1]) + (parts[2] + parts[3])
    average = totals[0] / (GROUPS * MEM)
    mean[...] = widen(average)
    innovation[...] = widen(totals[1] - average).astype(BF16)
    for m in range(MEM):
        out[m, :, :] = widen(scores[m] - average).astype(BF16)


def perturb_call(scores, parts):
    return pl.pallas_call(
        perturb_kernel,
        out_shape=(
            jax.ShapeDtypeStruct((MEM, OBS, WIDE), BF16),
            jax.ShapeDtypeStruct((OBS, WIDE), BF16),
            jax.ShapeDtypeStruct((OBS, WIDE), F32),
        ),
        in_specs=[VMEM] * 2,
        out_specs=(VMEM,) * 3,
        compiler_params=params(),
        name="perturb",
    )(scores, parts)


def gram_kernel(place, targets, loc, precision, innov, own, n1, n2, p2, out, every, rows, acc):
    group, core = place[0], place[1]
    for o in range(OBS):
        for lane in range(WIDE // 128):
            rows[lane, o * SPAN + 80 : (o + 1) * SPAN, :] = jnp.zeros((SPAN - 80, 128), F32)
    acc[...] = jnp.zeros_like(acc)
    after, before = MEM, 3 * MEM + 1
    at1 = before + core * (after - before)
    at2 = after + core * (before - after)
    for at, block in ((0, own), (at1, n1), (at2, n2), (2 * MEM, p2)):
        for m in range(MEM):
            wide = block[m].astype(F32)
            for g in range(OBS // 8):
                for lane in range(WIDE // 128):
                    rows[lane, pl.ds(g * 8 * SPAN + at + m, 8, stride=SPAN), :] = wide[
                        g * 8 : g * 8 + 8, lane * 128 : lane * 128 + 128
                    ]
    wide = innov[...].astype(F32)
    for g in range(OBS // 8):
        for lane in range(WIDE // 128):
            rows[lane, pl.ds(g * 8 * SPAN + 3 * MEM, 8, stride=SPAN), :] = wide[
                g * 8 : g * 8 + 8, lane * 128 : lane * 128 + 128
            ]
    live = lax.broadcasted_iota(jnp.int32, (24, 128), 0) < MEM
    fade = [
        jnp.where(live, precision[0:1, lane * 128 : lane * 128 + 128], 0.0)
        for lane in range(WIDE // 128)
    ]

    def footprint(o, carry):
        start = pl.multiple_of(o * SPAN, SPAN)
        result = None
        for lane in range(WIDE // 128):
            whole = rows[lane, pl.ds(start, SPAN), :]
            every[o, :, lane * 128 : lane * 128 + 128] = whole.astype(BF16)
            mine = whole[:24]
            weighted = jnp.concatenate(
                [mine * (loc[o * TOP + r] * fade[lane]) for r in range(TOP)], axis=0
            ).astype(BF16)
            right = jnp.concatenate([whole[:64], jnp.zeros((64, 128), F32)], axis=0).astype(BF16)
            term = lax.dot_general(weighted, right, NT, preferred_element_type=F32)
            result = term if result is None else result + term
        for r in range(TOP):
            index = targets[o * TOP + r]
            part = result[24 * r : 24 * r + 24]
            acc[index, 0:8, :] += part[0:8] + pltpu.roll(part[16:24], 64, 1)
            acc[index, 8:16, :] += part[8:16]
        return carry

    lax.fori_loop(0, OBS, footprint, 0, unroll=4)
    lane = lax.broadcasted_iota(jnp.int32, (8, 128), 1)
    row = lax.broadcasted_iota(jnp.int32, (8, 128), 0)
    column = lane % 64
    second = jnp.where(lane < 64, row * 0, 1)
    as_is = []
    for half in (second, jnp.where(row + 8 >= MEM // 2, 1, 0)):
        near = half == jnp.where(group >= GROUPS // 2, 1, 0)
        as_is.append((column < 40) | ((column < 50) & near))

    def pack(t, carry):
        top, middle = acc[t, 0:8, :], acc[t, 8:16, :]
        top = jnp.where(as_is[0], top, pltpu.roll(top, 118, 1))
        middle = jnp.where(as_is[1], middle, pltpu.roll(middle, 118, 1))
        low = top - top.astype(BF16).astype(F32)
        top = jnp.where(lane == 19, pltpu.roll(low, 97, 1), top)
        top = jnp.where(lane == 115, pltpu.roll(low, 1, 1), top)
        low = middle - middle.astype(BF16).astype(F32)
        middle = jnp.where(lane == 19, pltpu.roll(low, 97, 1), middle)
        tail = jnp.where(row < 4, pltpu.roll(top, 38, 1), pltpu.roll(pltpu.roll(top, 12, 1), 4, 0))
        out[t, :, :] = jnp.where(
            lane < SIDE, top, jnp.where(lane < 2 * SIDE, pltpu.roll(middle, SIDE, 1), tail)
        )
        return carry

    lax.fori_loop(0, 2 * CHIPS, pack, 0, unroll=8)


def gram_call(place, targets, loc, precision, innov, own, n1, n2, p2):
    packed = jax.ShapeDtypeStruct((2 * CHIPS, 8, 128), F32)
    return pl.pallas_call(
        gram_kernel,
        out_shape=(packed, jax.ShapeDtypeStruct((OBS, SPAN, WIDE), BF16)),
        in_specs=[SMEM] * 3 + [VMEM] * 6,
        out_specs=(VMEM,) * 2,
        scratch_shapes=[
            pltpu.VMEM((WIDE // 128, OBS * SPAN, 128), F32),
            pltpu.VMEM((2 * CHIPS, 16, 128), F32),
        ],
        compiler_params=params(),
        name="gram",
    )(place, targets, loc, precision, innov, own, n1, n2, p2)


def root_kernel(place, gathered, out, upper):
    group = place[0]
    order = GROUPS * MEM
    lane20 = lax.broadcasted_iota(jnp.int32, (MEM, 128), 1)
    row20 = lax.broadcasted_iota(jnp.int32, (MEM, 128), 0)
    lower = jnp.where(row20 >= MEM // 2, 1, 0)
    own = jnp.where((row20 < 16) & (lane20 == 19), 0.0, 0.5)
    own = jnp.where((row20 == 19) & (lane20 < 16), 1.0, own)
    lane8 = lax.broadcasted_iota(jnp.int32, (8, 128), 1)
    row8 = lax.broadcasted_iota(jnp.int32, (8, 128), 0)
    upper[...] = jnp.zeros_like(upper)
    for d in range(GROUPS):
        source = lax.rem(group + d, GROUPS)
        block = gathered[source]
        tail = jnp.where(
            lane8 < 26, pltpu.roll(block, 26, 1), pltpu.roll(pltpu.roll(block, 52, 1), 4, 0)
        )
        full = jnp.concatenate([block, pltpu.roll(block, 128 - SIDE, 1), tail[0:4]], axis=0)
        near = lower == jnp.where(source >= GROUPS // 2, 1, 0)
        scaled = jnp.where(lane20 < 20, own * full, full)
        scaled = jnp.where((lane20 < 40) | ((lane20 < 50) & near), scaled, 0.0)
        moved = jnp.where((lane20 >= 50) & (lane20 < 60) & ~near, pltpu.roll(full, 10, 1), 0.0)
        scaled = scaled + moved
        shift = MEM * d
        placed = scaled if d == 0 else pltpu.roll(scaled, shift, 1)
        placed = jnp.where(lane20 < order, placed, 0.0)
        if d >= 2:
            wrapped = pltpu.roll(scaled, (shift - order) % 128, 1)
            placed = placed + jnp.where(lane20 < shift - 20, wrapped, 0.0)
        low = jnp.where(
            row20 < 16, pltpu.roll(full, order - 19, 1), pltpu.roll(full, order - SIDE, 1)
        )
        pull = pltpu.roll(full, order - 50, 1) + low
        placed = placed + jnp.where(lane20 == order, pull, 0.0)
        upper[shift : shift + MEM, :] = placed
    half = upper[...]
    flipped = half.T
    row = lax.broadcasted_iota(jnp.int32, (128, 128), 0)
    lane = lax.broadcasted_iota(jnp.int32, (128, 128), 1)
    inside = (row < order) & (lane < order)
    identity = jnp.where(inside & (row == lane), 1.0, 0.0)
    symmetric = jnp.where(inside, half + flipped, 0.0)
    matrix = identity + symmetric / (order - 1.0)
    bound = jnp.max(jnp.sum(jnp.abs(matrix), axis=1, keepdims=True), axis=0, keepdims=True)
    pull = flipped[order : order + 8]
    pull = jnp.where(
        (lax.broadcasted_iota(jnp.int32, (8, 128), 1) < order)
        & (lax.broadcasted_iota(jnp.int32, (8, 128), 0) == 0),
        pull,
        0.0,
    )

    def times(a, b):
        return jnp.dot(a, b, precision=HIGHEST, preferred_element_type=F32)

    root = matrix / bound
    inverse = None
    for sweep in range(NS_ITERS):
        product = root if inverse is None else times(inverse, root)
        factor = 1.5 * identity - 0.5 * product
        if sweep < NS_ITERS - 1:
            root = times(root, factor)
        inverse = factor if inverse is None else times(factor, inverse)
    offset = times(times(pull, inverse), inverse) / (bound * (order - 1.0))
    weights = inverse[0:24] / jnp.sqrt(bound)
    offset = offset[0:1]
    own = (row[0:24] == lane[0:24]) & (row[0:24] < MEM)
    diagonal = jnp.sum(jnp.where(own, weights, 0.0), axis=0, keepdims=True)
    low = diagonal - diagonal.astype(BF16).astype(F32)
    offset_high = offset.astype(BF16).astype(F32)
    offset_low = offset - offset_high
    pair = [jnp.where(row8 == 1 + at, offset_low, 0.0) + jnp.where(row8 == 3 + at, offset_high, 0.0) for at in (0, 1)]
    low = jnp.where(row8 == 0, low, 0.0) + pair[0]
    low = jnp.where(lane8 >= 80, pltpu.roll(low, 80, 1), 0.0)
    low = low + jnp.where((lane8 >= 80) & (lane8 < 112), pltpu.roll(pair[1], 32, 1), 0.0)
    tail = jnp.where(row8 < 4, weights[16:24], 0.0)
    first = jnp.where(lane8 >= 80, pltpu.roll(tail, 80, 1), 0.0)
    second = jnp.where((lane8 >= 80) & (lane8 < 112), pltpu.roll(tail, 32, 1), 0.0)
    top = weights[0:8] + first + pltpu.roll(second, 4, 0)
    out[...] = jnp.concatenate([top, weights[8:16] + low], axis=0).astype(BF16)


def root_call(place, gathered):
    return pl.pallas_call(
        root_kernel,
        out_shape=jax.ShapeDtypeStruct((16, 128), BF16),
        in_specs=[SMEM, VMEM],
        out_specs=VMEM,
        scratch_shapes=[pltpu.VMEM((128, 128), F32)],
        compiler_params=params(),
        name="root",
    )(place, gathered)


def mix_kernel(place, targets, coef, mine, other, every, mean, out, rows):
    core = place[1]
    lane8 = lax.broadcasted_iota(jnp.int32, (8, 128), 1)
    row8 = lax.broadcasted_iota(jnp.int32, (8, 128), 0)

    def footprint(o, carry):
        blend = jnp.zeros((16, 128), F32)
        for r in range(TOP):
            target = targets[o * TOP + r]
            index = lax.div(target, 2)
            local = lax.rem(target, 2) == core
            piece = jnp.where(local, mine[index].astype(F32), other[index].astype(F32))
            blend = blend + coef[o * TOP + r] * piece
        top, middle = blend[0:8], blend[8:16]
        first = jnp.where(lane8 < 48, pltpu.roll(top, 48, 1), 0.0)
        second = jnp.where((lane8 >= 48) & (lane8 < 80), pltpu.roll(top, 96, 1), 0.0)
        tail = jnp.where(row8 < 4, first + pltpu.roll(second, 4, 0), 0.0)
        whole = jnp.concatenate(
            [jnp.where(lane8 < 80, top, 0.0), jnp.where(lane8 < 80, middle, 0.0), tail], axis=0
        )
        lane24 = lax.broadcasted_iota(jnp.int32, (24, 128), 1)
        own = lax.broadcasted_iota(jnp.int32, (24, 128), 0) == lane24
        left, right = pltpu.roll(middle, 48, 1), pltpu.roll(middle, 96, 1)
        offset = jnp.where(
            lane8[0:1] < 48,
            left[1:2] + left[3:4],
            jnp.where(lane8[0:1] < 80, right[2:3] + right[4:5], 0.0),
        )
        whole = whole + offset + jnp.where(own & (lane24 < MEM), left[0:1], 0.0)
        moved = jnp.where((lane24 > 60) & (lane24 < 81), pltpu.roll(whole, 1, 1), 0.0)
        whole = jnp.where(lane24 < 60, whole, moved)
        high = whole.astype(BF16).astype(F32)
        both = jnp.concatenate([high, whole - high], axis=0).astype(BF16)
        pert = jnp.concatenate([every[o], jnp.zeros((128 - SPAN, WIDE), BF16)], axis=0)
        mixed = jnp.dot(both, pert, preferred_element_type=F32)
        mixed = mixed[0:24] + mixed[24:48] + mean[pl.ds(o, 1), :]
        for g in range(3):
            for lane in range(WIDE // 128):
                rows[lane, pl.ds(g * 8 * OBS + o, 8, stride=OBS), :] = mixed[
                    g * 8 : g * 8 + 8, lane * 128 : lane * 128 + 128
                ]
        return carry

    lax.fori_loop(0, OBS, footprint, 0, unroll=4)
    for m in range(MEM):
        wide = jnp.concatenate(
            [rows[lane, m * OBS : (m + 1) * OBS, :] for lane in range(WIDE // 128)], axis=1
        )
        out[m, :, :] = wide[:, :COMPS].astype(BF16)


def mix_call(place, targets, coef, mine, other, every, mean):
    return pl.pallas_call(
        mix_kernel,
        out_shape=jax.ShapeDtypeStruct((MEM, OBS, COMPS), BF16),
        in_specs=[SMEM] * 3 + [VMEM] * 4,
        out_specs=VMEM,
        scratch_shapes=[pltpu.VMEM((WIDE // 128, 24 * OBS, 128), F32)],
        compiler_params=params(),
        name="mix",
    )(place, targets, coef, mine, other, every, mean)


def swap(value):
    return lax.ppermute(value, "core", [(0, 1), (1, 0)])


def turn(value, step=1):
    pairs = [(i, (i + step) % GROUPS) for i in range(GROUPS)]
    pairs += [(GROUPS + i, GROUPS + (i - step) % GROUPS) for i in range(GROUPS)]
    return lax.ppermute(value, ("core", "mem"), pairs)


def to_groups(value):
    copies = jnp.broadcast_to(value[None], (GROUPS,) + value.shape)
    return lax.all_to_all(copies, "mem", split_axis=0, concat_axis=0, tiled=True)


def pad_lanes(value, width):
    return jnp.pad(value, [(0, 0)] * (value.ndim - 1) + [(0, width - value.shape[-1])])


def body(radiance, observed, basis, precision_pc, tile_lists, radius_bins):
    group = lax.axis_index("mem")
    core = lax.axis_index("core")
    place = jnp.stack([group, core]).astype(jnp.int32)
    rad = jnp.transpose(radiance, (1, 0, 2)).reshape(MEM * OBS, GROUPS * BLOCK)

    turned = basis.T
    spare = ROWS - COMPS
    own = jnp.where(
        lax.rem(group, 2) == 1,
        jnp.pad(turned, ((0, spare), (FRAME - BLOCK, 0))),
        jnp.pad(turned, ((0, spare), (0, FRAME - BLOCK))),
    )
    beside1 = turn(own)
    first = own_call(place, rad, own)
    obs_partial = pad_lanes(jnp.dot(observed, basis, preferred_element_type=F32), ROWS)
    beside1, first, obs_partial = lax.optimization_barrier((beside1, first, obs_partial))
    far1 = turn(lax.dynamic_slice_in_dim(beside1, core * (ROWS - HALF), HALF, 0))
    scores, member_sum = scores_call(
        place, rad, first, beside1, swap(beside1), far1, swap(far1)
    )
    parts = to_groups(jnp.stack([member_sum, obs_partial]))
    perturbed, innovation, mean = perturb_call(scores, parts)
    next1 = turn(perturbed)
    next2 = turn(perturbed, -1)
    across = turn(next1)

    weights_loc = localization(radius_bins)
    rounded_loc = lax.reduce_precision(weights_loc, 8, 7).reshape(OBS * TOP)
    coef = (weights_loc / jnp.sum(weights_loc, axis=1, keepdims=True)).reshape(OBS * TOP)
    targets = tile_lists.reshape(OBS * TOP)
    packed, every = gram_call(
        place,
        targets,
        rounded_loc,
        pad_lanes(precision_pc[None], WIDE),
        innovation,
        perturbed,
        next1,
        next2,
        across,
    )
    arrived = lax.all_to_all(
        packed.astype(BF16), ("y", "z", "core"), split_axis=0, concat_axis=0, tiled=True
    )
    gathered = to_groups(jnp.sum(arrived.astype(F32), axis=0))
    weights = root_call(place, gathered)
    mine = lax.all_to_all(
        jnp.broadcast_to(weights[None], (CHIPS, 16, 128)),
        ("y", "z"),
        split_axis=0,
        concat_axis=0,
        tiled=True,
    )
    other = swap(mine)
    analysis = mix_call(place, targets, coef, mine, other, every, mean)
    return jnp.transpose(analysis, (1, 0, 2))


def solution(mesh):
    fine = Mesh(mesh.devices.reshape(8, 8, 2, GROUPS), ("y", "z", "core", "mem"))
    tile = ("y", "z", "core")
    placed = (
        P(tile, "mem", None),
        P(tile, "mem"),
        P("mem", None),
        P(),
        P(tile, None),
        P(tile, None),
    )
    return jax.shard_map(
        body, mesh=fine, in_specs=placed, out_specs=P(tile, "mem", None), check_vma=False
    )
```

```python
import jax
import jax.numpy as jnp
import numpy as np
from jax import lax
from jax.experimental import pallas as pl
from jax.experimental.pallas import tpu as pltpu
from jax.sharding import Mesh, PartitionSpec as P

NS_ITERS = 4
bin_spread = 3.0

GROUPS = 4
MEM = 20
OBS = 24
TOP = 3
COMPS = 300
WIDE = 384
ROWS = 304
HALF = 160
SIDE = 51
SPREAD = 64
SPAN = 96
BLOCK = 1088
FRAME = 1152
CHIPS = 64

F32 = jnp.float32
BF16 = jnp.bfloat16
HIGHEST = lax.Precision.HIGHEST
NT = (((1,), (1,)), ((), ()))
VMEM = pl.BlockSpec(memory_space=pltpu.VMEM)
SMEM = pl.BlockSpec(memory_space=pltpu.SMEM)
ANY = pl.BlockSpec(memory_space=pl.ANY)


def params():
    return pltpu.CompilerParams(vmem_limit_bytes=32 * 1024 * 1024)


def localization(radius_bins):
    scaled = radius_bins.astype(F32) / bin_spread
    return jnp.exp(-0.5 * scaled * scaled)


def frame_of(block):
    return pl.multiple_of(1024 * block + 128 * lax.div(block, 2), 128)


def own_kernel(place, rad, own, out):
    columns = pl.ds(frame_of(place[0]), FRAME)
    out[...] = lax.dot_general(rad[:, columns], own[...], NT, preferred_element_type=F32)


def own_call(place, rad, own):
    return pl.pallas_call(
        own_kernel,
        out_shape=jax.ShapeDtypeStruct((MEM * OBS, ROWS), F32),
        in_specs=[SMEM, VMEM, VMEM],
        out_specs=VMEM,
        compiler_params=params(),
        name="scores_own",
    )(place, rad, own)


def scores_kernel(place, rad, first, beside1, beside2, far1, far2, out, total, far):
    group, core = place[0], place[1]
    near = pl.ds(pl.multiple_of(core * (ROWS - HALF), 16), HALF)
    far[near, :] = far1[...]
    rest = ROWS - HALF
    source = pl.ds(pl.multiple_of((1 - core) * (HALF - rest), 16), rest)
    target = pl.ds(pl.multiple_of((1 - core) * HALF, 16), rest)
    far[target, :] = far2[source, :]
    step = 2 * core - 1
    blocks = (
        (beside1, lax.rem(group + step + GROUPS, GROUPS)),
        (beside2, lax.rem(group - step + GROUPS, GROUPS)),
        (far, lax.rem(group + 2, GROUPS)),
    )
    members = 10
    rows = members * OBS
    sums = jnp.zeros((OBS, ROWS), F32)
    for part in range(MEM // members):
        span = slice(part * rows, (part + 1) * rows)
        acc = first[span, :]
        for block, index in blocks:
            acc = acc + lax.dot_general(
                rad[span, pl.ds(frame_of(index), FRAME)],
                block[...],
                NT,
                preferred_element_type=F32,
            )
        block = acc.reshape(members, OBS, ROWS)
        out[part * members : (part + 1) * members, :, :] = block
        sums = sums + jnp.sum(block, axis=0)
    total[...] = sums


def scores_call(place, rad, first, *pieces):
    return pl.pallas_call(
        scores_kernel,
        out_shape=(
            jax.ShapeDtypeStruct((MEM, OBS, ROWS), F32),
            jax.ShapeDtypeStruct((OBS, ROWS), F32),
        ),
        in_specs=[SMEM] + [VMEM] * 6,
        out_specs=(VMEM, VMEM),
        scratch_shapes=[pltpu.VMEM((ROWS, FRAME), BF16)],
        compiler_params=params(),
        name="scores",
    )(place, rad, first, *pieces)


def widen(value):
    return jnp.concatenate([value, jnp.zeros(value.shape[:-1] + (WIDE - ROWS,), F32)], axis=-1)


def perturb_kernel(scores, parts, out, innovation, mean):
    totals = (parts[0] + parts[1]) + (parts[2] + parts[3])
    average = totals[0] / (GROUPS * MEM)
    mean[...] = widen(average)
    innovation[...] = widen(totals[1] - average).astype(BF16)
    for m in range(MEM):
        out[m, :, :] = widen(scores[m] - average).astype(BF16)


def perturb_call(scores, parts):
    return pl.pallas_call(
        perturb_kernel,
        out_shape=(
            jax.ShapeDtypeStruct((MEM, OBS, WIDE), BF16),
            jax.ShapeDtypeStruct((OBS, WIDE), BF16),
            jax.ShapeDtypeStruct((OBS, WIDE), F32),
        ),
        in_specs=[VMEM] * 2,
        out_specs=(VMEM,) * 3,
        compiler_params=params(),
        name="perturb",
    )(scores, parts)


def lay(rows, stride, at, block):
    for g in range(OBS // 8):
        for lane in range(WIDE // 128):
            rows[lane, pl.ds(g * 8 * stride + at, 8, stride=stride), :] = block[
                g * 8 : g * 8 + 8, lane * 128 : lane * 128 + 128
            ]


def lay_kernel(place, own, n1, n2, rows):
    core = place[1]
    for o in range(OBS):
        for lane in range(WIDE // 128):
            rows[lane, o * SPREAD + 56 : (o + 1) * SPREAD, :] = jnp.zeros((8, 128), F32)
    after, before = MEM, 2 * MEM
    at1 = before + core * (after - before)
    at2 = after + core * (before - after)
    for at, block in ((0, own), (at1, n1), (at2, n2)):
        for m in range(MEM):
            lay(rows, SPREAD, at + m, block[m].astype(F32))


def lay_call(place, own, n1, n2):
    return pl.pallas_call(
        lay_kernel,
        out_shape=jax.ShapeDtypeStruct((WIDE // 128, OBS * SPREAD, 128), F32),
        in_specs=[SMEM] + [VMEM] * 3,
        out_specs=VMEM,
        compiler_params=params(),
        cost_estimate=pl.CostEstimate(flops=1000000, bytes_accessed=6000000, transcendentals=0),
        name="lay",
    )(place, own, n1, n2)


def pack_maps():
    variants = []
    for first_half in (0, 1):
        kept = [
            list(range(40)) + list(range(40 + 10 * half, 50 + 10 * half)) + [60]
            for half in (first_half, 1 - first_half)
        ]
        maps = np.zeros((6, 128, 128), np.float32)
        for at, source in enumerate(kept[0]):
            if at != 19:
                maps[0:2, source, at] = 1
                maps[2, source, SIDE + at] = 1
        for at, source in enumerate(kept[1]):
            maps[at // 26, 64 + source, 102 + at % 26] = 1
            if at != 19:
                maps[3, source, SIDE + at] = 1
        maps[4, 60, 19] = maps[4, 124, 127] = maps[5, 60, SIDE + 19] = 1
        variants.append(maps.reshape(6 * 128, 128))
    return variants


def gram_kernel(targets, loc, precision, maps, innov, rows, p2, out, every, far, acc):
    acc[...] = jnp.zeros_like(acc)
    for o in range(OBS):
        for lane in range(WIDE // 128):
            far[lane, o * 24 + 16 : (o + 1) * 24, :] = jnp.zeros((8, 128), F32)
    for m in range(MEM):
        lay(far, 24, m, p2[m].astype(F32))
    lay(far, 24, MEM, innov[...].astype(F32))
    row = lax.broadcasted_iota(jnp.int32, (8, 128), 0)
    lane = lax.broadcasted_iota(jnp.int32, (8, 128), 1)

    def footprint(o, carry):
        start = pl.multiple_of(o * SPREAD, SPREAD)
        far_start = pl.multiple_of(o * 24, 24)
        result = None
        for at in range(WIDE // 128):
            span = slice(at * 128, at * 128 + 128)
            near = rows[at, pl.ds(start, SPREAD), :]
            whole = jnp.concatenate(
                [
                    near[:40],
                    far[at, pl.ds(far_start, 24), :],
                    near[40:],
                    jnp.zeros((SPAN - 24 - SPREAD, 128), F32),
                ],
                axis=0,
            )
            every[o, :, span] = whole.astype(BF16)
            last = jnp.where(row < 4, whole[16:24], pltpu.roll(whole[16:24], 4, 0))
            mine = jnp.concatenate([whole[:16], last], axis=0)
            weighted = jnp.concatenate(
                [mine * (loc[o * TOP + r] * precision[0:1, span]) for r in range(TOP)], axis=0
            ).astype(BF16)
            right = jnp.concatenate([whole[:64], whole[:64]], axis=0).astype(BF16)
            term = lax.dot_general(weighted, right, NT, preferred_element_type=F32)
            result = term if result is None else result + term
        for r in range(TOP):
            index = targets[o * TOP + r]
            part = result[24 * r : 24 * r + 24]
            acc[index, 0:8, :] += jnp.where(lane < 64, part[0:8], part[16:24])
            acc[index, 8:16, :] += part[8:16]
        return carry

    lax.fori_loop(0, OBS, footprint, 0, unroll=4)
    for t in range(0, 2 * CHIPS, 16):
        top, middle = acc[t : t + 16, 0:8, :], acc[t : t + 16, 8:16, :]
        low_top = top - top.astype(BF16).astype(F32)
        low_middle = middle - middle.astype(BF16).astype(F32)
        pieces = (
            jnp.where(row < 4, top, 0.0),
            jnp.where(row < 4, 0.0, top),
            jnp.where(row < 2, middle, 0.0),
            jnp.where(row < 2, 0.0, middle),
            jnp.where((row < 4) & (lane >= 64), 0.0, low_top),
            low_middle,
        )
        left = jnp.concatenate([p.reshape(128, 128).astype(BF16) for p in pieces], axis=1)
        packed = jnp.dot(left, maps[...], preferred_element_type=F32)
        out[t : t + 16, :, :] = packed.reshape(16, 8, 128)


def gram_call(targets, loc, precision, maps, innov, rows, p2):
    packed = jax.ShapeDtypeStruct((2 * CHIPS, 8, 128), F32)
    return pl.pallas_call(
        gram_kernel,
        out_shape=(packed, jax.ShapeDtypeStruct((OBS, SPAN, WIDE), BF16)),
        in_specs=[SMEM] * 2 + [VMEM] * 5,
        out_specs=(VMEM,) * 2,
        scratch_shapes=[
            pltpu.VMEM((WIDE // 128, OBS * 24, 128), F32),
            pltpu.VMEM((2 * CHIPS, 16, 128), F32),
        ],
        compiler_params=params(),
        name="gram",
    )(targets, loc, precision, maps, innov, rows, p2)


def root_kernel(place, gathered, out, upper):
    group = place[0]
    order = GROUPS * MEM
    lane20 = lax.broadcasted_iota(jnp.int32, (MEM, 128), 1)
    row20 = lax.broadcasted_iota(jnp.int32, (MEM, 128), 0)
    lower = jnp.where(row20 >= MEM // 2, 1, 0)
    own = jnp.where((row20 < 16) & (lane20 == 19), 0.0, 0.5)
    own = jnp.where((row20 == 19) & (lane20 < 16), 1.0, own)
    lane8 = lax.broadcasted_iota(jnp.int32, (8, 128), 1)
    row8 = lax.broadcasted_iota(jnp.int32, (8, 128), 0)
    upper[...] = jnp.zeros_like(upper)
    for d in range(GROUPS):
        source = lax.rem(group + d, GROUPS)
        block = gathered[source]
        tail = jnp.where(
            lane8 < 26, pltpu.roll(block, 26, 1), pltpu.roll(pltpu.roll(block, 52, 1), 4, 0)
        )
        full = jnp.concatenate([block, pltpu.roll(block, 128 - SIDE, 1), tail[0:4]], axis=0)
        near = lower == jnp.where(source >= GROUPS // 2, 1, 0)
        scaled = jnp.where(lane20 < 20, own * full, full)
        scaled = jnp.where((lane20 < 40) | ((lane20 < 50) & near), scaled, 0.0)
        moved = jnp.where((lane20 >= 50) & (lane20 < 60) & ~near, pltpu.roll(full, 10, 1), 0.0)
        scaled = scaled + moved
        shift = MEM * d
        placed = scaled if d == 0 else pltpu.roll(scaled, shift, 1)
        placed = jnp.where(lane20 < order, placed, 0.0)
        if d >= 2:
            wrapped = pltpu.roll(scaled, (shift - order) % 128, 1)
            placed = placed + jnp.where(lane20 < shift - 20, wrapped, 0.0)
        low = jnp.where(
            row20 < 16, pltpu.roll(full, order - 19, 1), pltpu.roll(full, order - SIDE, 1)
        )
        pull = pltpu.roll(full, order - 50, 1) + low
        placed = placed + jnp.where(lane20 == order, pull, 0.0)
        upper[shift : shift + MEM, :] = placed
    half = upper[...]
    flipped = half.T
    row = lax.broadcasted_iota(jnp.int32, (128, 128), 0)
    lane = lax.broadcasted_iota(jnp.int32, (128, 128), 1)
    inside = (row < order) & (lane < order)
    identity = jnp.where(inside & (row == lane), 1.0, 0.0)
    symmetric = jnp.where(inside, half + flipped, 0.0)
    matrix = identity + symmetric / (order - 1.0)
    bound = jnp.max(jnp.sum(jnp.abs(matrix), axis=1, keepdims=True), axis=0, keepdims=True)
    pull = flipped[order : order + 8]
    pull = jnp.where(
        (lax.broadcasted_iota(jnp.int32, (8, 128), 1) < order)
        & (lax.broadcasted_iota(jnp.int32, (8, 128), 0) == 0),
        pull,
        0.0,
    )

    def times(a, b):
        return jnp.dot(a, b, precision=HIGHEST, preferred_element_type=F32)

    root = matrix / bound
    inverse = None
    for sweep in range(NS_ITERS):
        product = root if inverse is None else times(inverse, root)
        factor = 1.5 * identity - 0.5 * product
        if sweep < NS_ITERS - 1:
            root = times(root, factor)
        inverse = factor if inverse is None else times(factor, inverse)
    offset = times(times(pull, inverse), inverse) / (bound * (order - 1.0))
    weights = inverse[0:24] / jnp.sqrt(bound)
    offset = offset[0:1]
    own = (row[0:24] == lane[0:24]) & (row[0:24] < MEM)
    diagonal = jnp.sum(jnp.where(own, weights, 0.0), axis=0, keepdims=True)
    low = diagonal - diagonal.astype(BF16).astype(F32)
    offset_high = offset.astype(BF16).astype(F32)
    offset_low = offset - offset_high
    pair = [jnp.where(row8 == 1 + at, offset_low, 0.0) + jnp.where(row8 == 3 + at, offset_high, 0.0) for at in (0, 1)]
    low = jnp.where(row8 == 0, low, 0.0) + pair[0]
    low = jnp.where(lane8 >= 80, pltpu.roll(low, 80, 1), 0.0)
    low = low + jnp.where((lane8 >= 80) & (lane8 < 112), pltpu.roll(pair[1], 32, 1), 0.0)
    tail = jnp.where(row8 < 4, weights[16:24], 0.0)
    first = jnp.where(lane8 >= 80, pltpu.roll(tail, 80, 1), 0.0)
    second = jnp.where((lane8 >= 80) & (lane8 < 112), pltpu.roll(tail, 32, 1), 0.0)
    top = weights[0:8] + first + pltpu.roll(second, 4, 0)
    out[...] = jnp.concatenate([top, weights[8:16] + low], axis=0).astype(BF16)


def root_call(place, gathered):
    return pl.pallas_call(
        root_kernel,
        out_shape=jax.ShapeDtypeStruct((16, 128), BF16),
        in_specs=[SMEM, VMEM],
        out_specs=VMEM,
        scratch_shapes=[pltpu.VMEM((128, 128), F32)],
        compiler_params=params(),
        name="root",
    )(place, gathered)


def mix_kernel(place, targets, coef, mine, other, every, mean, out, rows):
    core = place[1]
    lane8 = lax.broadcasted_iota(jnp.int32, (8, 128), 1)
    row8 = lax.broadcasted_iota(jnp.int32, (8, 128), 0)

    def footprint(o, carry):
        blend = jnp.zeros((16, 128), F32)
        for r in range(TOP):
            target = targets[o * TOP + r]
            index = lax.div(target, 2)
            local = lax.rem(target, 2) == core
            piece = jnp.where(local, mine[index].astype(F32), other[index].astype(F32))
            blend = blend + coef[o * TOP + r] * piece
        top, middle = blend[0:8], blend[8:16]
        first = jnp.where(lane8 < 48, pltpu.roll(top, 48, 1), 0.0)
        second = jnp.where((lane8 >= 48) & (lane8 < 80), pltpu.roll(top, 96, 1), 0.0)
        tail = jnp.where(row8 < 4, first + pltpu.roll(second, 4, 0), 0.0)
        whole = jnp.concatenate(
            [jnp.where(lane8 < 80, top, 0.0), jnp.where(lane8 < 80, middle, 0.0), tail], axis=0
        )
        lane24 = lax.broadcasted_iota(jnp.int32, (24, 128), 1)
        own = lax.broadcasted_iota(jnp.int32, (24, 128), 0) == lane24
        left, right = pltpu.roll(middle, 48, 1), pltpu.roll(middle, 96, 1)
        offset = jnp.where(
            lane8[0:1] < 48,
            left[1:2] + left[3:4],
            jnp.where(lane8[0:1] < 80, right[2:3] + right[4:5], 0.0),
        )
        whole = whole + offset + jnp.where(own & (lane24 < MEM), left[0:1], 0.0)
        moved = jnp.where((lane24 >= 64) & (lane24 < 84), pltpu.roll(whole, 4, 1), 0.0)
        whole = jnp.where(lane24 < 60, whole, moved)
        high = whole.astype(BF16).astype(F32)
        both = jnp.concatenate([high, whole - high], axis=0).astype(BF16)
        pert = jnp.concatenate([every[o], jnp.zeros((128 - SPAN, WIDE), BF16)], axis=0)
        mixed = jnp.dot(both, pert, preferred_element_type=F32)
        mixed = mixed[0:24] + mixed[24:48] + mean[pl.ds(o, 1), :]
        for g in range(3):
            for lane in range(WIDE // 128):
                rows[lane, pl.ds(g * 8 * OBS + o, 8, stride=OBS), :] = mixed[
                    g * 8 : g * 8 + 8, lane * 128 : lane * 128 + 128
                ]
        return carry

    lax.fori_loop(0, OBS, footprint, 0, unroll=4)
    for m in range(MEM):
        wide = jnp.concatenate(
            [rows[lane, m * OBS : (m + 1) * OBS, :] for lane in range(WIDE // 128)], axis=1
        )
        out[m, :, :] = wide[:, :COMPS].astype(BF16)


def mix_call(place, targets, coef, mine, other, every, mean):
    return pl.pallas_call(
        mix_kernel,
        out_shape=jax.ShapeDtypeStruct((MEM, OBS, COMPS), BF16),
        in_specs=[SMEM] * 3 + [VMEM] * 4,
        out_specs=VMEM,
        scratch_shapes=[pltpu.VMEM((WIDE // 128, 24 * OBS, 128), F32)],
        compiler_params=params(),
        name="mix",
    )(place, targets, coef, mine, other, every, mean)


def swap(value):
    return lax.ppermute(value, "core", [(0, 1), (1, 0)])


def turn(value, step=1):
    pairs = [(i, (i + step) % GROUPS) for i in range(GROUPS)]
    pairs += [(GROUPS + i, GROUPS + (i - step) % GROUPS) for i in range(GROUPS)]
    return lax.ppermute(value, ("core", "mem"), pairs)


def to_groups(value):
    copies = jnp.broadcast_to(value[None], (GROUPS,) + value.shape)
    return lax.all_to_all(copies, "mem", split_axis=0, concat_axis=0, tiled=True)


def pad_lanes(value, width):
    return jnp.pad(value, [(0, 0)] * (value.ndim - 1) + [(0, width - value.shape[-1])])


def body(radiance, observed, basis, precision_pc, tile_lists, radius_bins):
    group = lax.axis_index("mem")
    core = lax.axis_index("core")
    place = jnp.stack([group, core]).astype(jnp.int32)
    rad = jnp.transpose(radiance, (1, 0, 2)).reshape(MEM * OBS, GROUPS * BLOCK)

    turned = basis.T
    spare = ROWS - COMPS
    own = jnp.where(
        lax.rem(group, 2) == 1,
        jnp.pad(turned, ((0, spare), (FRAME - BLOCK, 0))),
        jnp.pad(turned, ((0, spare), (0, FRAME - BLOCK))),
    )
    beside1 = turn(own)
    first = own_call(place, rad, own)
    obs_partial = pad_lanes(jnp.dot(observed, basis, preferred_element_type=F32), ROWS)
    beside1, first, obs_partial = lax.optimization_barrier((beside1, first, obs_partial))
    far1 = turn(lax.dynamic_slice_in_dim(beside1, core * (ROWS - HALF), HALF, 0))
    scores, member_sum = scores_call(
        place, rad, first, beside1, swap(beside1), far1, swap(far1)
    )
    parts = to_groups(jnp.stack([member_sum, obs_partial]))
    perturbed, innovation, mean = perturb_call(scores, parts)
    next1 = turn(perturbed)
    next2 = turn(perturbed, -1)
    across = turn(next1)

    weights_loc = localization(radius_bins)
    rounded_loc = lax.reduce_precision(weights_loc, 8, 7).reshape(OBS * TOP)
    coef = (weights_loc / jnp.sum(weights_loc, axis=1, keepdims=True)).reshape(OBS * TOP)
    targets = tile_lists.reshape(OBS * TOP)
    maps = jnp.where(group < GROUPS // 2, *(jnp.asarray(each, BF16) for each in pack_maps()))
    packed, every = gram_call(
        targets,
        rounded_loc,
        pad_lanes(precision_pc[None], WIDE),
        maps,
        innovation,
        lay_call(place, perturbed, next1, next2),
        across,
    )
    arrived = lax.all_to_all(
        packed.astype(BF16), ("y", "z", "core"), split_axis=0, concat_axis=0, tiled=True
    )
    gathered = to_groups(jnp.sum(arrived.astype(F32), axis=0))
    weights = root_call(place, gathered)
    mine = lax.all_to_all(
        jnp.broadcast_to(weights[None], (CHIPS, 16, 128)),
        ("y", "z"),
        split_axis=0,
        concat_axis=0,
        tiled=True,
    )
    other = swap(mine)
    analysis = mix_call(place, targets, coef, mine, other, every, mean)
    return jnp.transpose(analysis, (1, 0, 2))


def solution(mesh):
    fine = Mesh(mesh.devices.reshape(8, 8, 2, GROUPS), ("y", "z", "core", "mem"))
    tile = ("y", "z", "core")
    placed = (
        P(tile, "mem", None),
        P(tile, "mem"),
        P("mem", None),
        P(),
        P(tile, None),
        P(tile, None),
    )
    return jax.shard_map(
        body, mesh=fine, in_specs=placed, out_specs=P(tile, "mem", None), check_vma=False
    )
```

```python
import jax
import jax.numpy as jnp
import numpy as np
from jax import lax
from jax.experimental import pallas as pl
from jax.experimental.pallas import tpu as pltpu
from jax.sharding import Mesh, PartitionSpec as P

NS_ITERS = 4
bin_spread = 3.0

GROUPS = 4
MEM = 20
OBS = 24
TOP = 3
COMPS = 300
WIDE = 384
ROWS = 304
HALF = 160
SIDE = 51
SPREAD = 64
SPAN = 96
BLOCK = 1088
FRAME = 1152
CHIPS = 64

F32 = jnp.float32
BF16 = jnp.bfloat16
HIGHEST = lax.Precision.HIGHEST
NT = (((1,), (1,)), ((), ()))
VMEM = pl.BlockSpec(memory_space=pltpu.VMEM)
SMEM = pl.BlockSpec(memory_space=pltpu.SMEM)
ANY = pl.BlockSpec(memory_space=pl.ANY)


def params():
    return pltpu.CompilerParams(vmem_limit_bytes=32 * 1024 * 1024)


def localization(radius_bins):
    scaled = radius_bins.astype(F32) / bin_spread
    return jnp.exp(-0.5 * scaled * scaled)


def frame_of(block):
    return pl.multiple_of(1024 * block + 128 * lax.div(block, 2), 128)


def own_kernel(place, rad, own, out):
    columns = pl.ds(frame_of(place[0]), FRAME)
    out[...] = lax.dot_general(rad[:, columns], own[...], NT, preferred_element_type=F32)


def own_call(place, rad, own):
    return pl.pallas_call(
        own_kernel,
        out_shape=jax.ShapeDtypeStruct((MEM * OBS, ROWS), F32),
        in_specs=[SMEM, VMEM, VMEM],
        out_specs=VMEM,
        compiler_params=params(),
        name="scores_own",
    )(place, rad, own)


def scores_kernel(place, rad, first, beside1, beside2, far1, far2, out, total, far):
    group, core = place[0], place[1]
    near = pl.ds(pl.multiple_of(core * (ROWS - HALF), 16), HALF)
    far[near, :] = far1[...]
    rest = ROWS - HALF
    source = pl.ds(pl.multiple_of((1 - core) * (HALF - rest), 16), rest)
    target = pl.ds(pl.multiple_of((1 - core) * HALF, 16), rest)
    far[target, :] = far2[source, :]
    step = 2 * core - 1
    blocks = (
        (beside1, lax.rem(group + step + GROUPS, GROUPS)),
        (beside2, lax.rem(group - step + GROUPS, GROUPS)),
        (far, lax.rem(group + 2, GROUPS)),
    )
    members = 10
    rows = members * OBS
    sums = jnp.zeros((OBS, ROWS), F32)
    for part in range(MEM // members):
        span = slice(part * rows, (part + 1) * rows)
        acc = first[span, :]
        for block, index in blocks:
            acc = acc + lax.dot_general(
                rad[span, pl.ds(frame_of(index), FRAME)],
                block[...],
                NT,
                preferred_element_type=F32,
            )
        block = acc.reshape(members, OBS, ROWS)
        out[part * members : (part + 1) * members, :, :] = block
        sums = sums + jnp.sum(block, axis=0)
    total[...] = sums


def scores_call(place, rad, first, *pieces):
    return pl.pallas_call(
        scores_kernel,
        out_shape=(
            jax.ShapeDtypeStruct((MEM, OBS, ROWS), F32),
            jax.ShapeDtypeStruct((OBS, ROWS), F32),
        ),
        in_specs=[SMEM] + [VMEM] * 6,
        out_specs=(VMEM, VMEM),
        scratch_shapes=[pltpu.VMEM((ROWS, FRAME), BF16)],
        compiler_params=params(),
        name="scores",
    )(place, rad, first, *pieces)


def widen(value):
    return jnp.concatenate([value, jnp.zeros(value.shape[:-1] + (WIDE - ROWS,), F32)], axis=-1)


def perturb_kernel(scores, parts, out, innovation, mean):
    totals = (parts[0] + parts[1]) + (parts[2] + parts[3])
    average = totals[0] / (GROUPS * MEM)
    mean[...] = widen(average)
    innovation[...] = widen(totals[1] - average).astype(BF16)
    for m in range(MEM):
        out[m, :, :] = widen(scores[m] - average).astype(BF16)


def perturb_call(scores, parts):
    return pl.pallas_call(
        perturb_kernel,
        out_shape=(
            jax.ShapeDtypeStruct((MEM, OBS, WIDE), BF16),
            jax.ShapeDtypeStruct((OBS, WIDE), BF16),
            jax.ShapeDtypeStruct((OBS, WIDE), F32),
        ),
        in_specs=[VMEM] * 2,
        out_specs=(VMEM,) * 3,
        compiler_params=params(),
        name="perturb",
    )(scores, parts)


def lay(rows, stride, at, block):
    for g in range(OBS // 8):
        for lane in range(WIDE // 128):
            rows[lane, pl.ds(g * 8 * stride + at, 8, stride=stride), :] = block[
                g * 8 : g * 8 + 8, lane * 128 : lane * 128 + 128
            ]


def lay_kernel(place, own, n1, n2, rows):
    core = place[1]
    for o in range(OBS):
        for lane in range(WIDE // 128):
            rows[lane, o * SPREAD + 56 : (o + 1) * SPREAD, :] = jnp.zeros((8, 128), F32)
    after, before = MEM, 2 * MEM
    at1 = before + core * (after - before)
    at2 = after + core * (before - after)
    for at, block in ((0, own), (at1, n1), (at2, n2)):
        for m in range(MEM):
            lay(rows, SPREAD, at + m, block[m].astype(F32))


def lay_call(place, own, n1, n2):
    return pl.pallas_call(
        lay_kernel,
        out_shape=jax.ShapeDtypeStruct((WIDE // 128, OBS * SPREAD, 128), F32),
        in_specs=[SMEM] + [VMEM] * 3,
        out_specs=VMEM,
        compiler_params=params(),
        cost_estimate=pl.CostEstimate(flops=1000000, bytes_accessed=6000000, transcendentals=0),
        name="lay",
    )(place, own, n1, n2)


def pack_maps():
    variants = []
    for first_half in (0, 1):
        kept = [
            list(range(40)) + list(range(40 + 10 * half, 50 + 10 * half)) + [60]
            for half in (first_half, 1 - first_half)
        ]
        maps = np.zeros((6, 128, 128), np.float32)
        for at, source in enumerate(kept[0]):
            if at != 19:
                maps[0:2, source, at] = 1
                maps[2, source, SIDE + at] = 1
        for at, source in enumerate(kept[1]):
            maps[at // 26, 64 + source, 102 + at % 26] = 1
            if at != 19:
                maps[3, source, SIDE + at] = 1
        maps[4, 60, 19] = maps[4, 124, 127] = maps[5, 60, SIDE + 19] = 1
        variants.append(maps.reshape(6 * 128, 128))
    return variants


def gram_kernel(targets, loc, precision, maps, innov, rows, p2, out, every, far, acc):
    acc[...] = jnp.zeros_like(acc)
    for o in range(OBS):
        for lane in range(WIDE // 128):
            far[lane, o * 24 + 16 : (o + 1) * 24, :] = jnp.zeros((8, 128), F32)
    for m in range(MEM):
        lay(far, 24, m, p2[m].astype(F32))
    lay(far, 24, MEM, innov[...].astype(F32))
    row = lax.broadcasted_iota(jnp.int32, (8, 128), 0)
    lane = lax.broadcasted_iota(jnp.int32, (8, 128), 1)

    def footprint(o, carry):
        start = pl.multiple_of(o * SPREAD, SPREAD)
        far_start = pl.multiple_of(o * 24, 24)
        result = None
        for at in range(WIDE // 128):
            span = slice(at * 128, at * 128 + 128)
            near = rows[at, pl.ds(start, SPREAD), :]
            whole = jnp.concatenate(
                [
                    near[:40],
                    far[at, pl.ds(far_start, 24), :],
                    near[40:],
                    jnp.zeros((SPAN - 24 - SPREAD, 128), F32),
                ],
                axis=0,
            )
            every[o, :, span] = whole.astype(BF16)
            last = jnp.where(row < 4, whole[16:24], pltpu.roll(whole[16:24], 4, 0))
            mine = jnp.concatenate([whole[:16], last], axis=0)
            weighted = jnp.concatenate(
                [mine * (loc[o * TOP + r] * precision[0:1, span]) for r in range(TOP)], axis=0
            ).astype(BF16)
            right = jnp.concatenate([whole[:64], whole[:64]], axis=0).astype(BF16)
            term = lax.dot_general(weighted, right, NT, preferred_element_type=F32)
            result = term if result is None else result + term
        for r in range(TOP):
            index = targets[o * TOP + r]
            part = result[24 * r : 24 * r + 24]
            acc[index, 0:8, :] += jnp.where(lane < 64, part[0:8], part[16:24])
            acc[index, 8:16, :] += part[8:16]
        return carry

    lax.fori_loop(0, OBS, footprint, 0, unroll=8)
    for t in range(0, 2 * CHIPS, 16):
        top, middle = acc[t : t + 16, 0:8, :], acc[t : t + 16, 8:16, :]
        low_top = top - top.astype(BF16).astype(F32)
        low_middle = middle - middle.astype(BF16).astype(F32)
        pieces = (
            jnp.where(row < 4, top, 0.0),
            jnp.where(row < 4, 0.0, top),
            jnp.where(row < 2, middle, 0.0),
            jnp.where(row < 2, 0.0, middle),
            jnp.where((row < 4) & (lane >= 64), 0.0, low_top),
            low_middle,
        )
        left = jnp.concatenate([p.reshape(128, 128).astype(BF16) for p in pieces], axis=1)
        packed = jnp.dot(left, maps[...], preferred_element_type=F32)
        out[t : t + 16, :, :] = packed.reshape(16, 8, 128)


def gram_call(targets, loc, precision, maps, innov, rows, p2):
    packed = jax.ShapeDtypeStruct((2 * CHIPS, 8, 128), F32)
    return pl.pallas_call(
        gram_kernel,
        out_shape=(packed, jax.ShapeDtypeStruct((OBS, SPAN, WIDE), BF16)),
        in_specs=[SMEM] * 2 + [VMEM] * 5,
        out_specs=(VMEM,) * 2,
        scratch_shapes=[
            pltpu.VMEM((WIDE // 128, OBS * 24, 128), F32),
            pltpu.VMEM((2 * CHIPS, 16, 128), F32),
        ],
        compiler_params=params(),
        name="gram",
    )(targets, loc, precision, maps, innov, rows, p2)


def root_kernel(place, gathered, out, upper):
    group = place[0]
    order = GROUPS * MEM
    lane20 = lax.broadcasted_iota(jnp.int32, (MEM, 128), 1)
    row20 = lax.broadcasted_iota(jnp.int32, (MEM, 128), 0)
    lower = jnp.where(row20 >= MEM // 2, 1, 0)
    own = jnp.where((row20 < 16) & (lane20 == 19), 0.0, 0.5)
    own = jnp.where((row20 == 19) & (lane20 < 16), 1.0, own)
    lane8 = lax.broadcasted_iota(jnp.int32, (8, 128), 1)
    row8 = lax.broadcasted_iota(jnp.int32, (8, 128), 0)
    upper[...] = jnp.zeros_like(upper)
    for d in range(GROUPS):
        source = lax.rem(group + d, GROUPS)
        block = gathered[source]
        tail = jnp.where(
            lane8 < 26, pltpu.roll(block, 26, 1), pltpu.roll(pltpu.roll(block, 52, 1), 4, 0)
        )
        full = jnp.concatenate([block, pltpu.roll(block, 128 - SIDE, 1), tail[0:4]], axis=0)
        near = lower == jnp.where(source >= GROUPS // 2, 1, 0)
        scaled = jnp.where(lane20 < 20, own * full, full)
        scaled = jnp.where((lane20 < 40) | ((lane20 < 50) & near), scaled, 0.0)
        moved = jnp.where((lane20 >= 50) & (lane20 < 60) & ~near, pltpu.roll(full, 10, 1), 0.0)
        scaled = scaled + moved
        shift = MEM * d
        placed = scaled if d == 0 else pltpu.roll(scaled, shift, 1)
        placed = jnp.where(lane20 < order, placed, 0.0)
        if d >= 2:
            wrapped = pltpu.roll(scaled, (shift - order) % 128, 1)
            placed = placed + jnp.where(lane20 < shift - 20, wrapped, 0.0)
        low = jnp.where(
            row20 < 16, pltpu.roll(full, order - 19, 1), pltpu.roll(full, order - SIDE, 1)
        )
        pull = pltpu.roll(full, order - 50, 1) + low
        placed = placed + jnp.where(lane20 == order, pull, 0.0)
        upper[shift : shift + MEM, :] = placed
    half = upper[...]
    flipped = half.T
    row = lax.broadcasted_iota(jnp.int32, (128, 128), 0)
    lane = lax.broadcasted_iota(jnp.int32, (128, 128), 1)
    inside = (row < order) & (lane < order)
    identity = jnp.where(inside & (row == lane), 1.0, 0.0)
    symmetric = jnp.where(inside, half + flipped, 0.0)
    matrix = identity + symmetric / (order - 1.0)
    bound = jnp.max(jnp.sum(jnp.abs(matrix), axis=1, keepdims=True), axis=0, keepdims=True)
    pull = flipped[order : order + 8]
    pull = jnp.where(
        (lax.broadcasted_iota(jnp.int32, (8, 128), 1) < order)
        & (lax.broadcasted_iota(jnp.int32, (8, 128), 0) == 0),
        pull,
        0.0,
    )

    def times(a, b):
        return jnp.dot(a, b, precision=HIGHEST, preferred_element_type=F32)

    root = matrix / bound
    inverse = None
    for sweep in range(NS_ITERS):
        product = root if inverse is None else times(inverse, root)
        factor = 1.5 * identity - 0.5 * product
        if sweep < NS_ITERS - 1:
            root = times(root, factor)
        inverse = factor if inverse is None else times(factor, inverse)
    offset = times(times(pull, inverse), inverse) / (bound * (order - 1.0))
    weights = inverse[0:24] / jnp.sqrt(bound)
    offset = offset[0:1]
    own = (row[0:24] == lane[0:24]) & (row[0:24] < MEM)
    diagonal = jnp.sum(jnp.where(own, weights, 0.0), axis=0, keepdims=True)
    low = diagonal - diagonal.astype(BF16).astype(F32)
    offset_high = offset.astype(BF16).astype(F32)
    offset_low = offset - offset_high
    pair = [jnp.where(row8 == 1 + at, offset_low, 0.0) + jnp.where(row8 == 3 + at, offset_high, 0.0) for at in (0, 1)]
    low = jnp.where(row8 == 0, low, 0.0) + pair[0]
    low = jnp.where(lane8 >= 80, pltpu.roll(low, 80, 1), 0.0)
    low = low + jnp.where((lane8 >= 80) & (lane8 < 112), pltpu.roll(pair[1], 32, 1), 0.0)
    tail = jnp.where(row8 < 4, weights[16:24], 0.0)
    first = jnp.where(lane8 >= 80, pltpu.roll(tail, 80, 1), 0.0)
    second = jnp.where((lane8 >= 80) & (lane8 < 112), pltpu.roll(tail, 32, 1), 0.0)
    top = weights[0:8] + first + pltpu.roll(second, 4, 0)
    out[...] = jnp.concatenate([top, weights[8:16] + low], axis=0).astype(BF16)


def root_call(place, gathered):
    return pl.pallas_call(
        root_kernel,
        out_shape=jax.ShapeDtypeStruct((16, 128), BF16),
        in_specs=[SMEM, VMEM],
        out_specs=VMEM,
        scratch_shapes=[pltpu.VMEM((128, 128), F32)],
        compiler_params=params(),
        name="root",
    )(place, gathered)


def mix_kernel(place, targets, coef, mine, other, every, mean, out, rows):
    core = place[1]
    lane8 = lax.broadcasted_iota(jnp.int32, (8, 128), 1)
    row8 = lax.broadcasted_iota(jnp.int32, (8, 128), 0)

    def footprint(o, carry):
        blend = jnp.zeros((16, 128), F32)
        for r in range(TOP):
            target = targets[o * TOP + r]
            index = lax.div(target, 2)
            local = lax.rem(target, 2) == core
            piece = jnp.where(local, mine[index].astype(F32), other[index].astype(F32))
            blend = blend + coef[o * TOP + r] * piece
        top, middle = blend[0:8], blend[8:16]
        first = jnp.where(lane8 < 48, pltpu.roll(top, 48, 1), 0.0)
        second = jnp.where((lane8 >= 48) & (lane8 < 80), pltpu.roll(top, 96, 1), 0.0)
        tail = jnp.where(row8 < 4, first + pltpu.roll(second, 4, 0), 0.0)
        whole = jnp.concatenate(
            [jnp.where(lane8 < 80, top, 0.0), jnp.where(lane8 < 80, middle, 0.0), tail], axis=0
        )
        lane24 = lax.broadcasted_iota(jnp.int32, (24, 128), 1)
        own = lax.broadcasted_iota(jnp.int32, (24, 128), 0) == lane24
        left, right = pltpu.roll(middle, 48, 1), pltpu.roll(middle, 96, 1)
        offset = jnp.where(
            lane8[0:1] < 48,
            left[1:2] + left[3:4],
            jnp.where(lane8[0:1] < 80, right[2:3] + right[4:5], 0.0),
        )
        whole = whole + offset + jnp.where(own & (lane24 < MEM), left[0:1], 0.0)
        moved = jnp.where((lane24 >= 64) & (lane24 < 84), pltpu.roll(whole, 4, 1), 0.0)
        whole = jnp.where(lane24 < 60, whole, moved)
        high = whole.astype(BF16).astype(F32)
        both = jnp.concatenate([high, whole - high], axis=0).astype(BF16)
        pert = jnp.concatenate([every[o], jnp.zeros((128 - SPAN, WIDE), BF16)], axis=0)
        mixed = jnp.dot(both, pert, preferred_element_type=F32)
        mixed = mixed[0:24] + mixed[24:48] + mean[pl.ds(o, 1), :]
        for g in range(3):
            for lane in range(WIDE // 128):
                rows[lane, pl.ds(g * 8 * OBS + o, 8, stride=OBS), :] = mixed[
                    g * 8 : g * 8 + 8, lane * 128 : lane * 128 + 128
                ]
        return carry

    lax.fori_loop(0, OBS, footprint, 0, unroll=12)
    for m in range(MEM):
        wide = jnp.concatenate(
            [rows[lane, m * OBS : (m + 1) * OBS, :] for lane in range(WIDE // 128)], axis=1
        )
        out[m, :, :] = wide[:, :COMPS].astype(BF16)


def mix_call(place, targets, coef, mine, other, every, mean):
    return pl.pallas_call(
        mix_kernel,
        out_shape=jax.ShapeDtypeStruct((MEM, OBS, COMPS), BF16),
        in_specs=[SMEM] * 3 + [VMEM] * 4,
        out_specs=VMEM,
        scratch_shapes=[pltpu.VMEM((WIDE // 128, 24 * OBS, 128), F32)],
        compiler_params=params(),
        name="mix",
    )(place, targets, coef, mine, other, every, mean)


def swap(value):
    return lax.ppermute(value, "core", [(0, 1), (1, 0)])


def turn(value, step=1):
    pairs = [(i, (i + step) % GROUPS) for i in range(GROUPS)]
    pairs += [(GROUPS + i, GROUPS + (i - step) % GROUPS) for i in range(GROUPS)]
    return lax.ppermute(value, ("core", "mem"), pairs)


def to_groups(value):
    copies = jnp.broadcast_to(value[None], (GROUPS,) + value.shape)
    return lax.all_to_all(copies, "mem", split_axis=0, concat_axis=0, tiled=True)


def pad_lanes(value, width):
    return jnp.pad(value, [(0, 0)] * (value.ndim - 1) + [(0, width - value.shape[-1])])


def body(radiance, observed, basis, precision_pc, tile_lists, radius_bins):
    group = lax.axis_index("mem")
    core = lax.axis_index("core")
    place = jnp.stack([group, core]).astype(jnp.int32)
    rad = jnp.transpose(radiance, (1, 0, 2)).reshape(MEM * OBS, GROUPS * BLOCK)

    turned = basis.T
    spare = ROWS - COMPS
    own = jnp.where(
        lax.rem(group, 2) == 1,
        jnp.pad(turned, ((0, spare), (FRAME - BLOCK, 0))),
        jnp.pad(turned, ((0, spare), (0, FRAME - BLOCK))),
    )
    beside1 = turn(own)
    first = own_call(place, rad, own)
    obs_partial = pad_lanes(jnp.dot(observed, basis, preferred_element_type=F32), ROWS)
    beside1, first, obs_partial = lax.optimization_barrier((beside1, first, obs_partial))
    far1 = turn(lax.dynamic_slice_in_dim(beside1, core * (ROWS - HALF), HALF, 0))
    scores, member_sum = scores_call(
        place, rad, first, beside1, swap(beside1), far1, swap(far1)
    )
    parts = to_groups(jnp.stack([member_sum, obs_partial]))
    perturbed, innovation, mean = perturb_call(scores, parts)
    next1 = turn(perturbed)
    next2 = turn(perturbed, -1)
    across = turn(next1)

    weights_loc = localization(radius_bins)
    rounded_loc = lax.reduce_precision(weights_loc, 8, 7).reshape(OBS * TOP)
    coef = (weights_loc / jnp.sum(weights_loc, axis=1, keepdims=True)).reshape(OBS * TOP)
    targets = tile_lists.reshape(OBS * TOP)
    maps = jnp.where(group < GROUPS // 2, *(jnp.asarray(each, BF16) for each in pack_maps()))
    packed, every = gram_call(
        targets,
        rounded_loc,
        pad_lanes(precision_pc[None], WIDE),
        maps,
        innovation,
        lay_call(place, perturbed, next1, next2),
        across,
    )
    arrived = lax.all_to_all(
        packed.astype(BF16), ("y", "z", "core"), split_axis=0, concat_axis=0, tiled=True
    )
    gathered = to_groups(jnp.sum(arrived.astype(F32), axis=0))
    weights = root_call(place, gathered)
    mine = lax.all_to_all(
        jnp.broadcast_to(weights[None], (CHIPS, 16, 128)),
        ("y", "z"),
        split_axis=0,
        concat_axis=0,
        tiled=True,
    )
    other = swap(mine)
    analysis = mix_call(place, targets, coef, mine, other, every, mean)
    return jnp.transpose(analysis, (1, 0, 2))


def solution(mesh):
    fine = Mesh(mesh.devices.reshape(8, 8, 2, GROUPS), ("y", "z", "core", "mem"))
    tile = ("y", "z", "core")
    placed = (
        P(tile, "mem", None),
        P(tile, "mem"),
        P("mem", None),
        P(),
        P(tile, None),
        P(tile, None),
    )
    return jax.shard_map(
        body, mesh=fine, in_specs=placed, out_specs=P(tile, "mem", None), check_vma=False
    )
```

```python
import jax
import jax.numpy as jnp
import numpy as np
from jax import lax
from jax.experimental import pallas as pl
from jax.experimental.pallas import tpu as pltpu
from jax.sharding import Mesh, PartitionSpec as P

NS_ITERS = 4
bin_spread = 3.0

GROUPS = 4
MEM = 20
OBS = 24
TOP = 3
COMPS = 300
WIDE = 384
ROWS = 304
HALF = 160
SIDE = 51
SPREAD = 64
SPAN = 96
BLOCK = 1088
FRAME = 1152
CHIPS = 64

F32 = jnp.float32
BF16 = jnp.bfloat16
HIGHEST = lax.Precision.HIGHEST
NT = (((1,), (1,)), ((), ()))
VMEM = pl.BlockSpec(memory_space=pltpu.VMEM)
SMEM = pl.BlockSpec(memory_space=pltpu.SMEM)
ANY = pl.BlockSpec(memory_space=pl.ANY)


def params():
    return pltpu.CompilerParams(vmem_limit_bytes=32 * 1024 * 1024)


def localization(radius_bins):
    scaled = radius_bins.astype(F32) / bin_spread
    return jnp.exp(-0.5 * scaled * scaled)


def frame_of(block):
    return pl.multiple_of(1024 * block + 128 * lax.div(block, 2), 128)


def own_kernel(place, rad, own, out):
    columns = pl.ds(frame_of(place[0]), FRAME)
    out[...] = lax.dot_general(rad[:, columns], own[...], NT, preferred_element_type=F32)


def own_call(place, rad, own):
    return pl.pallas_call(
        own_kernel,
        out_shape=jax.ShapeDtypeStruct((MEM * OBS, ROWS), F32),
        in_specs=[SMEM, VMEM, VMEM],
        out_specs=VMEM,
        compiler_params=params(),
        name="scores_own",
    )(place, rad, own)


def scores_kernel(place, rad, first, beside1, beside2, far1, far2, out, total, far):
    group, core = place[0], place[1]
    near = pl.ds(pl.multiple_of(core * (ROWS - HALF), 16), HALF)
    far[near, :] = far1[...]
    rest = ROWS - HALF
    source = pl.ds(pl.multiple_of((1 - core) * (HALF - rest), 16), rest)
    target = pl.ds(pl.multiple_of((1 - core) * HALF, 16), rest)
    far[target, :] = far2[source, :]
    step = 2 * core - 1
    blocks = (
        (beside1, lax.rem(group + step + GROUPS, GROUPS)),
        (beside2, lax.rem(group - step + GROUPS, GROUPS)),
        (far, lax.rem(group + 2, GROUPS)),
    )
    members = 10
    rows = members * OBS
    sums = jnp.zeros((OBS, ROWS), F32)
    for part in range(MEM // members):
        span = slice(part * rows, (part + 1) * rows)
        acc = first[span, :]
        for block, index in blocks:
            acc = acc + lax.dot_general(
                rad[span, pl.ds(frame_of(index), FRAME)],
                block[...],
                NT,
                preferred_element_type=F32,
            )
        block = acc.reshape(members, OBS, ROWS)
        out[part * members : (part + 1) * members, :, :] = block
        sums = sums + jnp.sum(block, axis=0)
    total[...] = sums


def scores_call(place, rad, first, *pieces):
    return pl.pallas_call(
        scores_kernel,
        out_shape=(
            jax.ShapeDtypeStruct((MEM, OBS, ROWS), F32),
            jax.ShapeDtypeStruct((OBS, ROWS), F32),
        ),
        in_specs=[SMEM] + [VMEM] * 6,
        out_specs=(VMEM, VMEM),
        scratch_shapes=[pltpu.VMEM((ROWS, FRAME), BF16)],
        compiler_params=params(),
        name="scores",
    )(place, rad, first, *pieces)


def widen(value):
    return jnp.concatenate([value, jnp.zeros(value.shape[:-1] + (WIDE - ROWS,), F32)], axis=-1)


def perturb_kernel(scores, parts, out, innovation, mean):
    totals = (parts[0] + parts[1]) + (parts[2] + parts[3])
    average = totals[0] / (GROUPS * MEM)
    mean[...] = widen(average)
    innovation[...] = widen(totals[1] - average).astype(BF16)
    for m in range(MEM):
        out[m, :, :] = widen(scores[m] - average).astype(BF16)


def perturb_call(scores, parts):
    return pl.pallas_call(
        perturb_kernel,
        out_shape=(
            jax.ShapeDtypeStruct((MEM, OBS, WIDE), BF16),
            jax.ShapeDtypeStruct((OBS, WIDE), BF16),
            jax.ShapeDtypeStruct((OBS, WIDE), F32),
        ),
        in_specs=[VMEM] * 2,
        out_specs=(VMEM,) * 3,
        compiler_params=params(),
        name="perturb",
    )(scores, parts)


def lay(rows, stride, at, block):
    for g in range(OBS // 8):
        for lane in range(WIDE // 128):
            rows[lane, pl.ds(g * 8 * stride + at, 8, stride=stride), :] = block[
                g * 8 : g * 8 + 8, lane * 128 : lane * 128 + 128
            ]


def lay_kernel(place, own, n1, n2, rows):
    core = place[1]
    for o in range(OBS):
        for lane in range(WIDE // 128):
            rows[lane, o * SPREAD + 56 : (o + 1) * SPREAD, :] = jnp.zeros((8, 128), F32)
    after, before = MEM, 2 * MEM
    at1 = before + core * (after - before)
    at2 = after + core * (before - after)
    for at, block in ((0, own), (at1, n1), (at2, n2)):
        for m in range(MEM):
            lay(rows, SPREAD, at + m, block[m].astype(F32))


def lay_call(place, own, n1, n2):
    return pl.pallas_call(
        lay_kernel,
        out_shape=jax.ShapeDtypeStruct((WIDE // 128, OBS * SPREAD, 128), F32),
        in_specs=[SMEM] + [VMEM] * 3,
        out_specs=VMEM,
        compiler_params=params(),
        cost_estimate=pl.CostEstimate(flops=1000000, bytes_accessed=6000000, transcendentals=0),
        name="lay",
    )(place, own, n1, n2)


def pack_maps():
    variants = []
    for first_half in (0, 1):
        kept = [
            list(range(40)) + list(range(40 + 10 * half, 50 + 10 * half)) + [60]
            for half in (first_half, 1 - first_half)
        ]
        maps = np.zeros((6, 128, 128), np.float32)
        for at, source in enumerate(kept[0]):
            if at != 19:
                maps[0:2, source, at] = 1
                maps[2, source, SIDE + at] = 1
        for at, source in enumerate(kept[1]):
            maps[at // 26, 64 + source, 102 + at % 26] = 1
            if at != 19:
                maps[3, source, SIDE + at] = 1
        maps[4, 60, 19] = maps[4, 124, 127] = maps[5, 60, SIDE + 19] = 1
        variants.append(maps.reshape(6 * 128, 128))
    return variants


def gram_kernel(targets, loc, precision, maps, innov, rows, p2, out, every, far, acc):
    acc[...] = jnp.zeros_like(acc)
    for o in range(OBS):
        for lane in range(WIDE // 128):
            far[lane, o * 24 + 16 : (o + 1) * 24, :] = jnp.zeros((8, 128), F32)
    for m in range(MEM):
        lay(far, 24, m, p2[m].astype(F32))
    lay(far, 24, MEM, innov[...].astype(F32))
    row = lax.broadcasted_iota(jnp.int32, (8, 128), 0)
    lane = lax.broadcasted_iota(jnp.int32, (8, 128), 1)

    def footprint(o, carry):
        start = pl.multiple_of(o * SPREAD, SPREAD)
        far_start = pl.multiple_of(o * 24, 24)
        result = None
        for at in range(WIDE // 128):
            span = slice(at * 128, at * 128 + 128)
            near = rows[at, pl.ds(start, SPREAD), :]
            whole = jnp.concatenate(
                [
                    near[:40],
                    far[at, pl.ds(far_start, 24), :],
                    near[40:],
                    jnp.zeros((SPAN - 24 - SPREAD, 128), F32),
                ],
                axis=0,
            )
            every[o, :, span] = whole.astype(BF16)
            last = jnp.where(row < 4, whole[16:24], pltpu.roll(whole[16:24], 4, 0))
            mine = jnp.concatenate([whole[:16], last], axis=0)
            weighted = jnp.concatenate(
                [mine * (loc[o * TOP + r] * precision[0:1, span]) for r in range(TOP)], axis=0
            ).astype(BF16)
            right = jnp.concatenate([whole[:64], whole[:64]], axis=0).astype(BF16)
            term = lax.dot_general(weighted, right, NT, preferred_element_type=F32)
            result = term if result is None else result + term
        for r in range(TOP):
            index = targets[o * TOP + r]
            part = result[24 * r : 24 * r + 24]
            acc[index, 0:8, :] += jnp.where(lane < 64, part[0:8], part[16:24])
            acc[index, 8:16, :] += part[8:16]
        return carry

    lax.fori_loop(0, OBS, footprint, 0, unroll=12)
    for t in range(0, 2 * CHIPS, 16):
        top, middle = acc[t : t + 16, 0:8, :], acc[t : t + 16, 8:16, :]
        low_top = top - top.astype(BF16).astype(F32)
        low_middle = middle - middle.astype(BF16).astype(F32)
        pieces = (
            jnp.where(row < 4, top, 0.0),
            jnp.where(row < 4, 0.0, top),
            jnp.where(row < 2, middle, 0.0),
            jnp.where(row < 2, 0.0, middle),
            jnp.where((row < 4) & (lane >= 64), 0.0, low_top),
            low_middle,
        )
        left = jnp.concatenate([p.reshape(128, 128).astype(BF16) for p in pieces], axis=1)
        packed = jnp.dot(left, maps[...], preferred_element_type=F32)
        out[t : t + 16, :, :] = packed.reshape(16, 8, 128)


def gram_call(targets, loc, precision, maps, innov, rows, p2):
    packed = jax.ShapeDtypeStruct((2 * CHIPS, 8, 128), F32)
    return pl.pallas_call(
        gram_kernel,
        out_shape=(packed, jax.ShapeDtypeStruct((OBS, SPAN, WIDE), BF16)),
        in_specs=[SMEM] * 2 + [VMEM] * 5,
        out_specs=(VMEM,) * 2,
        scratch_shapes=[
            pltpu.VMEM((WIDE // 128, OBS * 24, 128), F32),
            pltpu.VMEM((2 * CHIPS, 16, 128), F32),
        ],
        compiler_params=params(),
        name="gram",
    )(targets, loc, precision, maps, innov, rows, p2)


def root_kernel(place, gathered, out, upper):
    group = place[0]
    order = GROUPS * MEM
    lane20 = lax.broadcasted_iota(jnp.int32, (MEM, 128), 1)
    row20 = lax.broadcasted_iota(jnp.int32, (MEM, 128), 0)
    lower = jnp.where(row20 >= MEM // 2, 1, 0)
    own = jnp.where((row20 < 16) & (lane20 == 19), 0.0, 0.5)
    own = jnp.where((row20 == 19) & (lane20 < 16), 1.0, own)
    lane8 = lax.broadcasted_iota(jnp.int32, (8, 128), 1)
    row8 = lax.broadcasted_iota(jnp.int32, (8, 128), 0)
    upper[...] = jnp.zeros_like(upper)
    for d in range(GROUPS):
        source = lax.rem(group + d, GROUPS)
        block = gathered[source]
        tail = jnp.where(
            lane8 < 26, pltpu.roll(block, 26, 1), pltpu.roll(pltpu.roll(block, 52, 1), 4, 0)
        )
        full = jnp.concatenate([block, pltpu.roll(block, 128 - SIDE, 1), tail[0:4]], axis=0)
        near = lower == jnp.where(source >= GROUPS // 2, 1, 0)
        scaled = jnp.where(lane20 < 20, own * full, full)
        scaled = jnp.where((lane20 < 40) | ((lane20 < 50) & near), scaled, 0.0)
        moved = jnp.where((lane20 >= 50) & (lane20 < 60) & ~near, pltpu.roll(full, 10, 1), 0.0)
        scaled = scaled + moved
        shift = MEM * d
        placed = scaled if d == 0 else pltpu.roll(scaled, shift, 1)
        placed = jnp.where(lane20 < order, placed, 0.0)
        if d >= 2:
            wrapped = pltpu.roll(scaled, (shift - order) % 128, 1)
            placed = placed + jnp.where(lane20 < shift - 20, wrapped, 0.0)
        low = jnp.where(
            row20 < 16, pltpu.roll(full, order - 19, 1), pltpu.roll(full, order - SIDE, 1)
        )
        pull = pltpu.roll(full, order - 50, 1) + low
        placed = placed + jnp.where(lane20 == order, pull, 0.0)
        upper[shift : shift + MEM, :] = placed
    half = upper[...]
    flipped = half.T
    row = lax.broadcasted_iota(jnp.int32, (128, 128), 0)
    lane = lax.broadcasted_iota(jnp.int32, (128, 128), 1)
    inside = (row < order) & (lane < order)
    identity = jnp.where(inside & (row == lane), 1.0, 0.0)
    symmetric = jnp.where(inside, half + flipped, 0.0)
    matrix = identity + symmetric / (order - 1.0)
    bound = jnp.max(jnp.sum(jnp.abs(matrix), axis=1, keepdims=True), axis=0, keepdims=True)
    pull = flipped[order : order + 8]
    pull = jnp.where(
        (lax.broadcasted_iota(jnp.int32, (8, 128), 1) < order)
        & (lax.broadcasted_iota(jnp.int32, (8, 128), 0) == 0),
        pull,
        0.0,
    )

    def times(a, b):
        return jnp.dot(a, b, precision=HIGHEST, preferred_element_type=F32)

    root = matrix / bound
    inverse = None
    for sweep in range(NS_ITERS):
        product = root if inverse is None else times(inverse, root)
        factor = 1.5 * identity - 0.5 * product
        if sweep < NS_ITERS - 1:
            root = times(root, factor)
        inverse = factor if inverse is None else times(factor, inverse)
    offset = times(times(pull, inverse), inverse) / (bound * (order - 1.0))
    weights = inverse[0:24] / jnp.sqrt(bound)
    offset = offset[0:1]
    own = (row[0:24] == lane[0:24]) & (row[0:24] < MEM)
    diagonal = jnp.sum(jnp.where(own, weights, 0.0), axis=0, keepdims=True)
    low = diagonal - diagonal.astype(BF16).astype(F32)
    offset_high = offset.astype(BF16).astype(F32)
    offset_low = offset - offset_high
    pair = [jnp.where(row8 == 1 + at, offset_low, 0.0) + jnp.where(row8 == 3 + at, offset_high, 0.0) for at in (0, 1)]
    low = jnp.where(row8 == 0, low, 0.0) + pair[0]
    low = jnp.where(lane8 >= 80, pltpu.roll(low, 80, 1), 0.0)
    low = low + jnp.where((lane8 >= 80) & (lane8 < 112), pltpu.roll(pair[1], 32, 1), 0.0)
    tail = jnp.where(row8 < 4, weights[16:24], 0.0)
    first = jnp.where(lane8 >= 80, pltpu.roll(tail, 80, 1), 0.0)
    second = jnp.where((lane8 >= 80) & (lane8 < 112), pltpu.roll(tail, 32, 1), 0.0)
    top = weights[0:8] + first + pltpu.roll(second, 4, 0)
    out[...] = jnp.concatenate([top, weights[8:16] + low], axis=0).astype(BF16)


def root_call(place, gathered):
    return pl.pallas_call(
        root_kernel,
        out_shape=jax.ShapeDtypeStruct((16, 128), BF16),
        in_specs=[SMEM, VMEM],
        out_specs=VMEM,
        scratch_shapes=[pltpu.VMEM((128, 128), F32)],
        compiler_params=params(),
        name="root",
    )(place, gathered)


def mix_kernel(place, targets, coef, mine, other, every, mean, out, rows):
    core = place[1]
    lane8 = lax.broadcasted_iota(jnp.int32, (8, 128), 1)
    row8 = lax.broadcasted_iota(jnp.int32, (8, 128), 0)

    def footprint(o, carry):
        blend = jnp.zeros((16, 128), F32)
        for r in range(TOP):
            target = targets[o * TOP + r]
            index = lax.div(target, 2)
            local = lax.rem(target, 2) == core
            piece = jnp.where(local, mine[index].astype(F32), other[index].astype(F32))
            blend = blend + coef[o * TOP + r] * piece
        top, middle = blend[0:8], blend[8:16]
        first = jnp.where(lane8 < 48, pltpu.roll(top, 48, 1), 0.0)
        second = jnp.where((lane8 >= 48) & (lane8 < 80), pltpu.roll(top, 96, 1), 0.0)
        tail = jnp.where(row8 < 4, first + pltpu.roll(second, 4, 0), 0.0)
        whole = jnp.concatenate(
            [jnp.where(lane8 < 80, top, 0.0), jnp.where(lane8 < 80, middle, 0.0), tail], axis=0
        )
        lane24 = lax.broadcasted_iota(jnp.int32, (24, 128), 1)
        own = lax.broadcasted_iota(jnp.int32, (24, 128), 0) == lane24
        left, right = pltpu.roll(middle, 48, 1), pltpu.roll(middle, 96, 1)
        offset = jnp.where(
            lane8[0:1] < 48,
            left[1:2] + left[3:4],
            jnp.where(lane8[0:1] < 80, right[2:3] + right[4:5], 0.0),
        )
        whole = whole + offset + jnp.where(own & (lane24 < MEM), left[0:1], 0.0)
        moved = jnp.where((lane24 >= 64) & (lane24 < 84), pltpu.roll(whole, 4, 1), 0.0)
        whole = jnp.where(lane24 < 60, whole, moved)
        high = whole.astype(BF16).astype(F32)
        both = jnp.concatenate([high, whole - high], axis=0).astype(BF16)
        pert = jnp.concatenate([every[o], jnp.zeros((128 - SPAN, WIDE), BF16)], axis=0)
        mixed = jnp.dot(both, pert, preferred_element_type=F32)
        mixed = mixed[0:24] + mixed[24:48] + mean[pl.ds(o, 1), :]
        for g in range(3):
            for lane in range(WIDE // 128):
                rows[lane, pl.ds(g * 8 * OBS + o, 8, stride=OBS), :] = mixed[
                    g * 8 : g * 8 + 8, lane * 128 : lane * 128 + 128
                ]
        return carry

    lax.fori_loop(0, OBS, footprint, 0, unroll=24)
    for m in range(MEM):
        wide = jnp.concatenate(
            [rows[lane, m * OBS : (m + 1) * OBS, :] for lane in range(WIDE // 128)], axis=1
        )
        out[m, :, :] = wide[:, :COMPS].astype(BF16)


def mix_call(place, targets, coef, mine, other, every, mean):
    return pl.pallas_call(
        mix_kernel,
        out_shape=jax.ShapeDtypeStruct((MEM, OBS, COMPS), BF16),
        in_specs=[SMEM] * 3 + [VMEM] * 4,
        out_specs=VMEM,
        scratch_shapes=[pltpu.VMEM((WIDE // 128, 24 * OBS, 128), F32)],
        compiler_params=params(),
        name="mix",
    )(place, targets, coef, mine, other, every, mean)


def swap(value):
    return lax.ppermute(value, "core", [(0, 1), (1, 0)])


def turn(value, step=1):
    pairs = [(i, (i + step) % GROUPS) for i in range(GROUPS)]
    pairs += [(GROUPS + i, GROUPS + (i - step) % GROUPS) for i in range(GROUPS)]
    return lax.ppermute(value, ("core", "mem"), pairs)


def to_groups(value):
    copies = jnp.broadcast_to(value[None], (GROUPS,) + value.shape)
    return lax.all_to_all(copies, "mem", split_axis=0, concat_axis=0, tiled=True)


def pad_lanes(value, width):
    return jnp.pad(value, [(0, 0)] * (value.ndim - 1) + [(0, width - value.shape[-1])])


def body(radiance, observed, basis, precision_pc, tile_lists, radius_bins):
    group = lax.axis_index("mem")
    core = lax.axis_index("core")
    place = jnp.stack([group, core]).astype(jnp.int32)
    rad = jnp.transpose(radiance, (1, 0, 2)).reshape(MEM * OBS, GROUPS * BLOCK)

    turned = basis.T
    spare = ROWS - COMPS
    edge = FRAME - BLOCK
    framed = jnp.pad(turned, ((0, spare), (edge, edge)))
    own = lax.dynamic_slice_in_dim(framed, edge * (1 - lax.rem(group, 2)), FRAME, 1)
    beside1 = turn(own)
    first = own_call(place, rad, own)
    obs_partial = pad_lanes(jnp.dot(observed, basis, preferred_element_type=F32), ROWS)
    beside1, first, obs_partial = lax.optimization_barrier((beside1, first, obs_partial))
    far1 = turn(lax.dynamic_slice_in_dim(beside1, core * (ROWS - HALF), HALF, 0))
    scores, member_sum = scores_call(
        place, rad, first, beside1, swap(beside1), far1, swap(far1)
    )
    parts = to_groups(jnp.stack([member_sum, obs_partial]))
    perturbed, innovation, mean = perturb_call(scores, parts)
    next1 = turn(perturbed)
    next2 = turn(perturbed, -1)
    across = turn(next1)

    weights_loc = localization(radius_bins)
    rounded_loc = lax.reduce_precision(weights_loc, 8, 7).reshape(OBS * TOP)
    coef = (weights_loc / jnp.sum(weights_loc, axis=1, keepdims=True)).reshape(OBS * TOP)
    targets = tile_lists.reshape(OBS * TOP)
    maps = jnp.where(group < GROUPS // 2, *(jnp.asarray(each, BF16) for each in pack_maps()))
    packed, every = gram_call(
        targets,
        rounded_loc,
        pad_lanes(precision_pc[None], WIDE),
        maps,
        innovation,
        lay_call(place, perturbed, next1, next2),
        across,
    )
    arrived = lax.all_to_all(
        packed.astype(BF16), ("y", "z", "core"), split_axis=0, concat_axis=0, tiled=True
    )
    gathered = to_groups(jnp.sum(arrived.astype(F32), axis=0))
    weights = root_call(place, gathered)
    mine = lax.all_to_all(
        jnp.broadcast_to(weights[None], (CHIPS, 16, 128)),
        ("y", "z"),
        split_axis=0,
        concat_axis=0,
        tiled=True,
    )
    other = swap(mine)
    analysis = mix_call(place, targets, coef, mine, other, every, mean)
    return jnp.transpose(analysis, (1, 0, 2))


def solution(mesh):
    fine = Mesh(mesh.devices.reshape(8, 8, 2, GROUPS), ("y", "z", "core", "mem"))
    tile = ("y", "z", "core")
    placed = (
        P(tile, "mem", None),
        P(tile, "mem"),
        P("mem", None),
        P(),
        P(tile, None),
        P(tile, None),
    )
    return jax.shard_map(
        body, mesh=fine, in_specs=placed, out_specs=P(tile, "mem", None), check_vma=False
    )
```

```python
import jax
import jax.numpy as jnp
import numpy as np
from jax import lax
from jax.experimental import pallas as pl
from jax.experimental.pallas import tpu as pltpu
from jax.sharding import Mesh, PartitionSpec as P

NS_ITERS = 4
bin_spread = 3.0

GROUPS = 4
MEM = 20
OBS = 24
TOP = 3
COMPS = 300
WIDE = 384
ROWS = 304
HALF = 160
SIDE = 51
SPREAD = 64
SPAN = 96
BLOCK = 1088
FRAME = 1152
CHIPS = 64

F32 = jnp.float32
BF16 = jnp.bfloat16
HIGHEST = lax.Precision.HIGHEST
NT = (((1,), (1,)), ((), ()))
VMEM = pl.BlockSpec(memory_space=pltpu.VMEM)
SMEM = pl.BlockSpec(memory_space=pltpu.SMEM)
ANY = pl.BlockSpec(memory_space=pl.ANY)


def params():
    return pltpu.CompilerParams(vmem_limit_bytes=32 * 1024 * 1024)


def localization(radius_bins):
    scaled = radius_bins.astype(F32) / bin_spread
    return jnp.exp(-0.5 * scaled * scaled)


def frame_of(block):
    return pl.multiple_of(1024 * block + 128 * lax.div(block, 2), 128)


def own_kernel(place, rad, own, out):
    columns = pl.ds(frame_of(place[0]), FRAME)
    out[...] = lax.dot_general(rad[:, columns], own[...], NT, preferred_element_type=F32)


def own_call(place, rad, own):
    return pl.pallas_call(
        own_kernel,
        out_shape=jax.ShapeDtypeStruct((MEM * OBS, ROWS), F32),
        in_specs=[SMEM, VMEM, VMEM],
        out_specs=VMEM,
        compiler_params=params(),
        name="scores_own",
    )(place, rad, own)


def scores_kernel(place, rad, first, beside1, beside2, far1, far2, out, total, far):
    group, core = place[0], place[1]
    near = pl.ds(pl.multiple_of(core * (ROWS - HALF), 16), HALF)
    far[near, :] = far1[...]
    rest = ROWS - HALF
    source = pl.ds(pl.multiple_of((1 - core) * (HALF - rest), 16), rest)
    target = pl.ds(pl.multiple_of((1 - core) * HALF, 16), rest)
    far[target, :] = far2[source, :]
    step = 2 * core - 1
    blocks = (
        (beside1, lax.rem(group + step + GROUPS, GROUPS)),
        (beside2, lax.rem(group - step + GROUPS, GROUPS)),
        (far, lax.rem(group + 2, GROUPS)),
    )
    members = 10
    rows = members * OBS
    sums = jnp.zeros((OBS, ROWS), F32)
    for part in range(MEM // members):
        span = slice(part * rows, (part + 1) * rows)
        acc = first[span, :]
        for block, index in blocks:
            acc = acc + lax.dot_general(
                rad[span, pl.ds(frame_of(index), FRAME)],
                block[...],
                NT,
                preferred_element_type=F32,
            )
        block = acc.reshape(members, OBS, ROWS)
        out[part * members : (part + 1) * members, :, :] = block
        sums = sums + jnp.sum(block, axis=0)
    total[...] = sums


def scores_call(place, rad, first, *pieces):
    return pl.pallas_call(
        scores_kernel,
        out_shape=(
            jax.ShapeDtypeStruct((MEM, OBS, ROWS), F32),
            jax.ShapeDtypeStruct((OBS, ROWS), F32),
        ),
        in_specs=[SMEM] + [VMEM] * 6,
        out_specs=(VMEM, VMEM),
        scratch_shapes=[pltpu.VMEM((ROWS, FRAME), BF16)],
        compiler_params=params(),
        name="scores",
    )(place, rad, first, *pieces)


def widen(value):
    return jnp.concatenate([value, jnp.zeros(value.shape[:-1] + (WIDE - ROWS,), F32)], axis=-1)


def perturb_kernel(scores, parts, out, innovation, mean):
    totals = (parts[0] + parts[1]) + (parts[2] + parts[3])
    average = totals[0] / (GROUPS * MEM)
    mean[...] = widen(average)
    innovation[...] = widen(totals[1] - average).astype(BF16)
    for m in range(MEM):
        out[m, :, :] = widen(scores[m] - average).astype(BF16)


def perturb_call(scores, parts):
    return pl.pallas_call(
        perturb_kernel,
        out_shape=(
            jax.ShapeDtypeStruct((MEM, OBS, WIDE), BF16),
            jax.ShapeDtypeStruct((OBS, WIDE), BF16),
            jax.ShapeDtypeStruct((OBS, WIDE), F32),
        ),
        in_specs=[VMEM] * 2,
        out_specs=(VMEM,) * 3,
        compiler_params=params(),
        name="perturb",
    )(scores, parts)


def lay(rows, stride, at, block):
    for g in range(OBS // 8):
        for lane in range(WIDE // 128):
            rows[lane, pl.ds(g * 8 * stride + at, 8, stride=stride), :] = block[
                g * 8 : g * 8 + 8, lane * 128 : lane * 128 + 128
            ]


def lay_kernel(place, own, n1, n2, rows):
    core = place[1]
    for o in range(OBS):
        for lane in range(WIDE // 128):
            rows[lane, o * SPREAD + 56 : (o + 1) * SPREAD, :] = jnp.zeros((8, 128), F32)
    after, before = MEM, 2 * MEM
    at1 = before + core * (after - before)
    at2 = after + core * (before - after)
    for at, block in ((0, own), (at1, n1), (at2, n2)):
        for m in range(MEM):
            lay(rows, SPREAD, at + m, block[m].astype(F32))


def lay_call(place, own, n1, n2):
    return pl.pallas_call(
        lay_kernel,
        out_shape=jax.ShapeDtypeStruct((WIDE // 128, OBS * SPREAD, 128), F32),
        in_specs=[SMEM] + [VMEM] * 3,
        out_specs=VMEM,
        compiler_params=params(),
        cost_estimate=pl.CostEstimate(flops=1000000, bytes_accessed=6000000, transcendentals=0),
        name="lay",
    )(place, own, n1, n2)


def pack_maps():
    variants = []
    for first_half in (0, 1):
        kept = [
            list(range(40)) + list(range(40 + 10 * half, 50 + 10 * half)) + [60]
            for half in (first_half, 1 - first_half)
        ]
        maps = np.zeros((6, 128, 128), np.float32)
        for at, source in enumerate(kept[0]):
            if at != 19:
                maps[0:2, source, at] = 1
                maps[2, source, SIDE + at] = 1
        for at, source in enumerate(kept[1]):
            maps[at // 26, 64 + source, 102 + at % 26] = 1
            if at != 19:
                maps[3, source, SIDE + at] = 1
        maps[4, 60, 19] = maps[4, 124, 127] = maps[5, 60, SIDE + 19] = 1
        variants.append(maps.reshape(6 * 128, 128))
    return variants


def gram_kernel(targets, loc, precision, maps, innov, rows, p2, out, every, far, acc):
    acc[...] = jnp.zeros_like(acc)
    for o in range(OBS):
        for lane in range(WIDE // 128):
            far[lane, o * 24 + 16 : (o + 1) * 24, :] = jnp.zeros((8, 128), F32)
    for m in range(MEM):
        lay(far, 24, m, p2[m].astype(F32))
    lay(far, 24, MEM, innov[...].astype(F32))
    row = lax.broadcasted_iota(jnp.int32, (8, 128), 0)
    lane = lax.broadcasted_iota(jnp.int32, (8, 128), 1)

    def footprint(o, carry):
        start = pl.multiple_of(o * SPREAD, SPREAD)
        far_start = pl.multiple_of(o * 24, 24)
        result = None
        for at in range(WIDE // 128):
            span = slice(at * 128, at * 128 + 128)
            near = rows[at, pl.ds(start, SPREAD), :]
            whole = jnp.concatenate(
                [
                    near[:40],
                    far[at, pl.ds(far_start, 24), :],
                    near[40:],
                    jnp.zeros((SPAN - 24 - SPREAD, 128), F32),
                ],
                axis=0,
            )
            every[o, :, span] = whole.astype(BF16)
            last = jnp.where(row < 4, whole[16:24], pltpu.roll(whole[16:24], 4, 0))
            mine = jnp.concatenate([whole[:16], last], axis=0)
            weighted = jnp.concatenate(
                [mine * (loc[o * TOP + r] * precision[0:1, span]) for r in range(TOP)], axis=0
            ).astype(BF16)
            right = jnp.concatenate([whole[:64], whole[:64]], axis=0).astype(BF16)
            term = lax.dot_general(weighted, right, NT, preferred_element_type=F32)
            result = term if result is None else result + term
        for r in range(TOP):
            index = targets[o * TOP + r]
            part = result[24 * r : 24 * r + 24]
            acc[index, 0:8, :] += jnp.where(lane < 64, part[0:8], part[16:24])
            acc[index, 8:16, :] += part[8:16]
        return carry

    lax.fori_loop(0, OBS, footprint, 0, unroll=12)
    for t in range(0, 2 * CHIPS, 16):
        top, middle = acc[t : t + 16, 0:8, :], acc[t : t + 16, 8:16, :]
        low_top = top - top.astype(BF16).astype(F32)
        low_middle = middle - middle.astype(BF16).astype(F32)
        pieces = (
            jnp.where(row < 4, top, 0.0),
            jnp.where(row < 4, 0.0, top),
            jnp.where(row < 2, middle, 0.0),
            jnp.where(row < 2, 0.0, middle),
            jnp.where((row < 4) & (lane >= 64), 0.0, low_top),
            low_middle,
        )
        left = jnp.concatenate([p.reshape(128, 128).astype(BF16) for p in pieces], axis=1)
        packed = jnp.dot(left, maps[...], preferred_element_type=F32)
        out[t : t + 16, :, :] = packed.reshape(16, 8, 128).astype(BF16)


def gram_call(targets, loc, precision, maps, innov, rows, p2):
    packed = jax.ShapeDtypeStruct((2 * CHIPS, 8, 128), BF16)
    return pl.pallas_call(
        gram_kernel,
        out_shape=(packed, jax.ShapeDtypeStruct((OBS, SPAN, WIDE), BF16)),
        in_specs=[SMEM] * 2 + [VMEM] * 5,
        out_specs=(VMEM,) * 2,
        scratch_shapes=[
            pltpu.VMEM((WIDE // 128, OBS * 24, 128), F32),
            pltpu.VMEM((2 * CHIPS, 16, 128), F32),
        ],
        compiler_params=params(),
        name="gram",
    )(targets, loc, precision, maps, innov, rows, p2)


def root_kernel(place, gathered, out, upper):
    group = place[0]
    order = GROUPS * MEM
    lane20 = lax.broadcasted_iota(jnp.int32, (MEM, 128), 1)
    row20 = lax.broadcasted_iota(jnp.int32, (MEM, 128), 0)
    lower = jnp.where(row20 >= MEM // 2, 1, 0)
    own = jnp.where((row20 < 16) & (lane20 == 19), 0.0, 0.5)
    own = jnp.where((row20 == 19) & (lane20 < 16), 1.0, own)
    lane8 = lax.broadcasted_iota(jnp.int32, (8, 128), 1)
    row8 = lax.broadcasted_iota(jnp.int32, (8, 128), 0)
    upper[...] = jnp.zeros_like(upper)
    for d in range(GROUPS):
        source = lax.rem(group + d, GROUPS)
        block = gathered[source]
        tail = jnp.where(
            lane8 < 26, pltpu.roll(block, 26, 1), pltpu.roll(pltpu.roll(block, 52, 1), 4, 0)
        )
        full = jnp.concatenate([block, pltpu.roll(block, 128 - SIDE, 1), tail[0:4]], axis=0)
        near = lower == jnp.where(source >= GROUPS // 2, 1, 0)
        scaled = jnp.where(lane20 < 20, own * full, full)
        scaled = jnp.where((lane20 < 40) | ((lane20 < 50) & near), scaled, 0.0)
        moved = jnp.where((lane20 >= 50) & (lane20 < 60) & ~near, pltpu.roll(full, 10, 1), 0.0)
        scaled = scaled + moved
        shift = MEM * d
        placed = scaled if d == 0 else pltpu.roll(scaled, shift, 1)
        placed = jnp.where(lane20 < order, placed, 0.0)
        if d >= 2:
            wrapped = pltpu.roll(scaled, (shift - order) % 128, 1)
            placed = placed + jnp.where(lane20 < shift - 20, wrapped, 0.0)
        low = jnp.where(
            row20 < 16, pltpu.roll(full, order - 19, 1), pltpu.roll(full, order - SIDE, 1)
        )
        pull = pltpu.roll(full, order - 50, 1) + low
        placed = placed + jnp.where(lane20 == order, pull, 0.0)
        upper[shift : shift + MEM, :] = placed
    half = upper[...]
    flipped = half.T
    row = lax.broadcasted_iota(jnp.int32, (128, 128), 0)
    lane = lax.broadcasted_iota(jnp.int32, (128, 128), 1)
    inside = (row < order) & (lane < order)
    identity = jnp.where(inside & (row == lane), 1.0, 0.0)
    symmetric = jnp.where(inside, half + flipped, 0.0)
    matrix = identity + symmetric / (order - 1.0)
    bound = jnp.max(jnp.sum(jnp.abs(matrix), axis=1, keepdims=True), axis=0, keepdims=True)
    pull = flipped[order : order + 8]
    pull = jnp.where(
        (lax.broadcasted_iota(jnp.int32, (8, 128), 1) < order)
        & (lax.broadcasted_iota(jnp.int32, (8, 128), 0) == 0),
        pull,
        0.0,
    )

    def times(a, b):
        return jnp.dot(a, b, precision=HIGHEST, preferred_element_type=F32)

    root = matrix / bound
    inverse = None
    for sweep in range(NS_ITERS):
        product = root if inverse is None else times(inverse, root)
        factor = 1.5 * identity - 0.5 * product
        if sweep < NS_ITERS - 1:
            root = times(root, factor)
        inverse = factor if inverse is None else times(factor, inverse)
    offset = times(times(pull, inverse), inverse) / (bound * (order - 1.0))
    weights = inverse[0:24] / jnp.sqrt(bound)
    offset = offset[0:1]
    own = (row[0:24] == lane[0:24]) & (row[0:24] < MEM)
    diagonal = jnp.sum(jnp.where(own, weights, 0.0), axis=0, keepdims=True)
    low = diagonal - diagonal.astype(BF16).astype(F32)
    offset_high = offset.astype(BF16).astype(F32)
    offset_low = offset - offset_high
    pair = [jnp.where(row8 == 1 + at, offset_low, 0.0) + jnp.where(row8 == 3 + at, offset_high, 0.0) for at in (0, 1)]
    low = jnp.where(row8 == 0, low, 0.0) + pair[0]
    low = jnp.where(lane8 >= 80, pltpu.roll(low, 80, 1), 0.0)
    low = low + jnp.where((lane8 >= 80) & (lane8 < 112), pltpu.roll(pair[1], 32, 1), 0.0)
    tail = jnp.where(row8 < 4, weights[16:24], 0.0)
    first = jnp.where(lane8 >= 80, pltpu.roll(tail, 80, 1), 0.0)
    second = jnp.where((lane8 >= 80) & (lane8 < 112), pltpu.roll(tail, 32, 1), 0.0)
    top = weights[0:8] + first + pltpu.roll(second, 4, 0)
    out[...] = jnp.concatenate([top, weights[8:16] + low], axis=0).astype(BF16)


def root_call(place, gathered):
    return pl.pallas_call(
        root_kernel,
        out_shape=jax.ShapeDtypeStruct((16, 128), BF16),
        in_specs=[SMEM, VMEM],
        out_specs=VMEM,
        scratch_shapes=[pltpu.VMEM((128, 128), F32)],
        compiler_params=params(),
        name="root",
    )(place, gathered)


def mix_kernel(place, targets, coef, mine, other, every, mean, out, rows):
    core = place[1]
    lane8 = lax.broadcasted_iota(jnp.int32, (8, 128), 1)
    row8 = lax.broadcasted_iota(jnp.int32, (8, 128), 0)

    def footprint(o, carry):
        blend = jnp.zeros((16, 128), F32)
        for r in range(TOP):
            target = targets[o * TOP + r]
            index = lax.div(target, 2)
            local = lax.rem(target, 2) == core
            piece = jnp.where(local, mine[index].astype(F32), other[index].astype(F32))
            blend = blend + coef[o * TOP + r] * piece
        top, middle = blend[0:8], blend[8:16]
        first = jnp.where(lane8 < 48, pltpu.roll(top, 48, 1), 0.0)
        second = jnp.where((lane8 >= 48) & (lane8 < 80), pltpu.roll(top, 96, 1), 0.0)
        tail = jnp.where(row8 < 4, first + pltpu.roll(second, 4, 0), 0.0)
        whole = jnp.concatenate(
            [jnp.where(lane8 < 80, top, 0.0), jnp.where(lane8 < 80, middle, 0.0), tail], axis=0
        )
        lane24 = lax.broadcasted_iota(jnp.int32, (24, 128), 1)
        own = lax.broadcasted_iota(jnp.int32, (24, 128), 0) == lane24
        left, right = pltpu.roll(middle, 48, 1), pltpu.roll(middle, 96, 1)
        offset = jnp.where(
            lane8[0:1] < 48,
            left[1:2] + left[3:4],
            jnp.where(lane8[0:1] < 80, right[2:3] + right[4:5], 0.0),
        )
        whole = whole + offset + jnp.where(own & (lane24 < MEM), left[0:1], 0.0)
        moved = jnp.where((lane24 >= 64) & (lane24 < 84), pltpu.roll(whole, 4, 1), 0.0)
        whole = jnp.where(lane24 < 60, whole, moved)
        high = whole.astype(BF16).astype(F32)
        both = jnp.concatenate([high, whole - high], axis=0).astype(BF16)
        pert = jnp.concatenate([every[o], jnp.zeros((128 - SPAN, WIDE), BF16)], axis=0)
        mixed = jnp.dot(both, pert, preferred_element_type=F32)
        mixed = mixed[0:24] + mixed[24:48] + mean[pl.ds(o, 1), :]
        for g in range(3):
            for lane in range(WIDE // 128):
                rows[lane, pl.ds(g * 8 * OBS + o, 8, stride=OBS), :] = mixed[
                    g * 8 : g * 8 + 8, lane * 128 : lane * 128 + 128
                ]
        return carry

    lax.fori_loop(0, OBS, footprint, 0, unroll=24)
    for m in range(MEM):
        wide = jnp.concatenate(
            [rows[lane, m * OBS : (m + 1) * OBS, :] for lane in range(WIDE // 128)], axis=1
        )
        out[m, :, :] = wide[:, :COMPS].astype(BF16)


def mix_call(place, targets, coef, mine, other, every, mean):
    return pl.pallas_call(
        mix_kernel,
        out_shape=jax.ShapeDtypeStruct((MEM, OBS, COMPS), BF16),
        in_specs=[SMEM] * 3 + [VMEM] * 4,
        out_specs=VMEM,
        scratch_shapes=[pltpu.VMEM((WIDE // 128, 24 * OBS, 128), F32)],
        compiler_params=params(),
        name="mix",
    )(place, targets, coef, mine, other, every, mean)


def swap(value):
    return lax.ppermute(value, "core", [(0, 1), (1, 0)])


def turn(value, step=1):
    pairs = [(i, (i + step) % GROUPS) for i in range(GROUPS)]
    pairs += [(GROUPS + i, GROUPS + (i - step) % GROUPS) for i in range(GROUPS)]
    return lax.ppermute(value, ("core", "mem"), pairs)


def to_groups(value):
    copies = jnp.broadcast_to(value[None], (GROUPS,) + value.shape)
    return lax.all_to_all(copies, "mem", split_axis=0, concat_axis=0, tiled=True)


def pad_lanes(value, width):
    return jnp.pad(value, [(0, 0)] * (value.ndim - 1) + [(0, width - value.shape[-1])])


def body(radiance, observed, basis, precision_pc, tile_lists, radius_bins):
    group = lax.axis_index("mem")
    core = lax.axis_index("core")
    place = jnp.stack([group, core]).astype(jnp.int32)
    rad = jnp.transpose(radiance, (1, 0, 2)).reshape(MEM * OBS, GROUPS * BLOCK)

    turned = basis.T
    spare = ROWS - COMPS
    edge = FRAME - BLOCK
    framed = jnp.pad(turned, ((0, spare), (edge, edge)))
    own = lax.dynamic_slice_in_dim(framed, edge * (1 - lax.rem(group, 2)), FRAME, 1)
    beside1 = turn(own)
    first = own_call(place, rad, own)
    obs_partial = pad_lanes(jnp.dot(observed, basis, preferred_element_type=F32), ROWS)
    beside1, first, obs_partial = lax.optimization_barrier((beside1, first, obs_partial))
    far1 = turn(lax.dynamic_slice_in_dim(beside1, core * (ROWS - HALF), HALF, 0))
    scores, member_sum = scores_call(
        place, rad, first, beside1, swap(beside1), far1, swap(far1)
    )
    parts = to_groups(jnp.stack([member_sum, obs_partial]))
    perturbed, innovation, mean = perturb_call(scores, parts)
    next1 = turn(perturbed)
    next2 = turn(perturbed, -1)
    across = turn(next1)

    weights_loc = localization(radius_bins)
    rounded_loc = lax.reduce_precision(weights_loc, 8, 7).reshape(OBS * TOP)
    coef = (weights_loc / jnp.sum(weights_loc, axis=1, keepdims=True)).reshape(OBS * TOP)
    targets = tile_lists.reshape(OBS * TOP)
    maps = jnp.where(group < GROUPS // 2, *(jnp.asarray(each, BF16) for each in pack_maps()))
    packed, every = gram_call(
        targets,
        rounded_loc,
        pad_lanes(precision_pc[None], WIDE),
        maps,
        innovation,
        lay_call(place, perturbed, next1, next2),
        across,
    )
    arrived = lax.all_to_all(
        packed, ("y", "z", "core"), split_axis=0, concat_axis=0, tiled=True
    )
    gathered = to_groups(jnp.sum(arrived.astype(F32), axis=0))
    weights = root_call(place, gathered)
    mine = lax.all_to_all(
        jnp.broadcast_to(weights[None], (CHIPS, 16, 128)),
        ("y", "z"),
        split_axis=0,
        concat_axis=0,
        tiled=True,
    )
    other = swap(mine)
    analysis = mix_call(place, targets, coef, mine, other, every, mean)
    return jnp.transpose(analysis, (1, 0, 2))


def solution(mesh):
    fine = Mesh(mesh.devices.reshape(8, 8, 2, GROUPS), ("y", "z", "core", "mem"))
    tile = ("y", "z", "core")
    placed = (
        P(tile, "mem", None),
        P(tile, "mem"),
        P("mem", None),
        P(),
        P(tile, None),
        P(tile, None),
    )
    return jax.shard_map(
        body, mesh=fine, in_specs=placed, out_specs=P(tile, "mem", None), check_vma=False
    )
```
